256 devices in a mesh: head: 4 (over y), seq: 32 (over z, x_hi, core), dp: 2 (over x_lo).
Axes of the slice: x: 4 (x_hi: 2, x_lo: 2; x = x_hi * 2 + x_lo), y: 4, z: 8, core: 2. Of those that a mesh axis runs over, the one named last changes fastest.
Arguments:
- trunk: bfloat16 [2, 4096, 5120], P('dp', 'seq'), may hold values from -6 to 6
- gains: float32 [4, 5120], P('head'), may hold values from 0.1 to 1.9
- queries: bfloat16 [4, 2, 4096, 2560], P('head', 'dp', 'seq'), may hold values from -5 to 5
- keys: bfloat16 [4, 2, 4096, 512], P('head', 'dp', 'seq'), may hold values from -5 to 5
- values: bfloat16 [4, 2, 4096, 512], P('head', 'dp', 'seq'), may hold values from -6 to 6
- outputs: bfloat16 [4, 2, 4096, 2560], P('head', 'dp', 'seq'), may hold values from -3 to 3
- out_grad: bfloat16 [4, 2, 4096, 2560], P('head', 'dp', 'seq'), may hold values from -6 to 6
- kv_weight: bfloat16 [4, 5120, 1024], P('head', 'seq'), may hold values from -0.078125 to 0.078125
Outputs:
- query_grad: bfloat16 [4, 2, 4096, 2560], P('head', 'dp', 'seq')
- trunk_grad: bfloat16 [2, 4096, 5120], P('dp', 'seq', 'head')
- gain_grad: float32 [4, 5120], P('head')
The draws below stay inside these ranges and needn't reach their ends.
All inputs are finite; a program needn't handle non-finite values.
Results may differ from the reference program's by a relative error of at most 0.025.
Values may be sent and summed in bfloat16 or wider, within the bound.
No kernel may reach another device: no remote copies, remote signals or barrier semaphores. Data moves between devices by JAX's collectives and lax.ppermute only.
A program may use at most 128 MiB of HBM per device.

```python
import math
import jax
import jax.numpy as jnp
from jax import lax

D = 5120
QH = 20
KVH = 4
MTP = 4
HD = 128
TOK_DEV = 128
LEN = 4096
SEQS = 2
N_SEQ = 32


def draw_queries(key, part):
    key = jax.random.fold_in(key, 7)
    base_key = jax.random.fold_in(key, 0)
    base = jax.random.normal(base_key, (MTP, SEQS, LEN, QH, HD), jnp.float32)
    base = jnp.clip(base, -5.0, 5.0)
    return base.reshape(MTP, SEQS, LEN, QH * HD).astype(jnp.bfloat16)


def draw_keys(key, part):
    key = jax.random.fold_in(key, 9)
    base_key = jax.random.fold_in(key, 0)
    base = jax.random.normal(base_key, (MTP, SEQS, LEN, KVH, HD), jnp.float32)
    base = jnp.clip(base, -5.0, 5.0)
    return base.reshape(MTP, SEQS, LEN, KVH * HD).astype(jnp.bfloat16)


def levels(stream_key, shape, cuts, least, high):
    factor_of = 1.0
    for dim, blocks in cuts:
        draws = jax.random.uniform(jax.random.fold_in(jax.random.fold_in(stream_key, 6), dim), (blocks,), jnp.float32, least / len(cuts), high / len(cuts))
        factor_of = factor_of * jnp.repeat(jnp.exp(draws), shape[dim] // blocks).reshape((-1,) + (1,) * (len(shape) - 1 - dim))
    return factor_of


def scatter_about(key, dims, width, limit, cuts=(), kind=jnp.bfloat16):
    level = levels(key, dims, cuts, -0.22, 0.18) if cuts else 1.0
    values = jax.random.normal(key, dims, jnp.float32) * width * level
    return jnp.minimum(jnp.maximum(values, -limit), limit).astype(kind)


def setup_inputs(seed: int = 0) -> dict:
    streams_of = jax.random.split(jax.random.key(seed), 9)
    trunk = scatter_about(streams_of[0], (SEQS, LEN, D), 1.0, 6.0, ((0, 2), (1, 32)))
    gains = jnp.clip(1.0 + 0.18 * jax.random.normal(streams_of[1], (MTP, D), jnp.float32), 0.1, 1.9)
    queries = draw_queries(jax.random.fold_in(streams_of[8], 71), 0)
    keys = draw_keys(jax.random.fold_in(streams_of[8], 71), 0)
    values = scatter_about(streams_of[4], (MTP, SEQS, LEN, KVH * HD), 1.0, 6.0, ((0, 4), (1, 2), (2, 32)))
    outputs = scatter_about(streams_of[5], (MTP, SEQS, LEN, QH * HD), 0.5, 3.0, ((0, 4), (1, 2), (2, 32)))
    out_grad = scatter_about(streams_of[6], (MTP, SEQS, LEN, QH * HD), 1.0, 6.0, ((0, 4), (1, 2), (2, 32)))
    kv_weight = scatter_about(streams_of[7], (MTP, D, 2 * KVH * HD), D ** -0.5, 0.078125, ((0, 4), (1, 32)))
    return dict(trunk=trunk, gains=gains, queries=queries, keys=keys, values=values, outputs=outputs, out_grad=out_grad, kv_weight=kv_weight)


def sequence_grads(query_seq, key_seq, value_seq, output_seq, grad_seq):
    group_size = QH // KVH
    score_scale = 1.0 / math.sqrt(HD)
    key_all = key_seq.astype(jnp.float32).reshape(LEN, KVH, HD)
    value_all = value_seq.astype(jnp.float32).reshape(LEN, KVH, HD)
    query_blocks = query_seq.astype(jnp.float32).reshape(N_SEQ, TOK_DEV, KVH, group_size, HD)
    grad_blocks = grad_seq.astype(jnp.float32).reshape(N_SEQ, TOK_DEV, KVH, group_size, HD)
    output_blocks = output_seq.astype(jnp.float32).reshape(N_SEQ, TOK_DEV, KVH, group_size, HD)
    key_pos = jnp.arange(LEN, dtype=jnp.int32)

    def block_step(running, inputs):
        query_block, grad_block, output_block, block_index = inputs
        query_pos = block_index * TOK_DEV + jnp.arange(TOK_DEV, dtype=jnp.int32)
        causal = key_pos[None, :] <= query_pos[:, None]
        scores = jnp.einsum('tgjd,ugd->gjtu', query_block, key_all) * score_scale
        scores = jnp.where(causal[None, None], scores, -jnp.inf)
        row_max = lax.optimization_barrier(jnp.max(scores, axis=-1, keepdims=True))
        exp_scores = jnp.exp(scores - row_max)
        probs_high = exp_scores / lax.optimization_barrier(jnp.sum(exp_scores, axis=-1, keepdims=True))
        probs_low = lax.optimization_barrier(probs_high.astype(jnp.bfloat16)).astype(jnp.float32)
        delta_rows = lax.optimization_barrier(jnp.sum(grad_block * output_block, axis=-1)).transpose(1, 2, 0)
        dprobs = jnp.einsum('tgjd,ugd->gjtu', grad_block, value_all)
        dscores = (probs_high * (dprobs - delta_rows[..., None]) * score_scale).astype(jnp.bfloat16)
        dscores = lax.optimization_barrier(dscores).astype(jnp.float32)
        query_grad = jnp.einsum('gjtu,ugd->tgjd', dscores, key_all).astype(jnp.bfloat16)
        key_grad = jnp.einsum('gjtu,tgjd->ugd', dscores, query_block).reshape(LEN, KVH * HD)
        value_grad = jnp.einsum('gjtu,tgjd->ugd', probs_low, grad_block).reshape(LEN, KVH * HD)
        partial_sum = jnp.concatenate([key_grad, value_grad], axis=1)
        partial_sum = lax.optimization_barrier(partial_sum.astype(jnp.bfloat16)).astype(jnp.float32)
        return (running + partial_sum, query_grad.reshape(TOK_DEV, QH * HD))
    running, query_grads = lax.scan(block_step, jnp.zeros((LEN, 2 * KVH * HD), jnp.float32), (query_blocks, grad_blocks, output_blocks, jnp.arange(N_SEQ, dtype=jnp.int32)))
    return (query_grads.reshape(LEN, QH * HD), running.astype(jnp.bfloat16))

def reference(trunk, gains, queries, keys, values, outputs, out_grad, kv_weight):
    query_list = []
    gain_list = []
    trunk_sums = [jnp.zeros((LEN, D), jnp.float32) for replica in range(SEQS)]
    for which in range(MTP):
        gain_sum = jnp.zeros((D,), jnp.float32)
        row_list = []
        for replica in range(SEQS):
            query_grad, kv_grad = sequence_grads(queries[which, replica], keys[which, replica], values[which, replica], outputs[which, replica], out_grad[which, replica])
            row_list.append(query_grad)
            proj = jnp.dot(kv_grad, kv_weight[which].T, preferred_element_type=jnp.float32)
            hidden = trunk[replica].astype(jnp.float32)
            inverse_rms = lax.rsqrt(lax.optimization_barrier(jnp.mean(hidden * hidden, axis=-1, keepdims=True)) + 1e-05)
            normed = hidden * inverse_rms
            gain_sum = gain_sum + lax.optimization_barrier(jnp.sum(proj * normed, axis=0))
            scaled = gains[which] * proj
            row_stat = lax.optimization_barrier(jnp.mean(normed * scaled, axis=-1, keepdims=True))
            trunk_sums[replica] = trunk_sums[replica] + (scaled - normed * row_stat) * inverse_rms
        query_list.append(jnp.stack(row_list))
        gain_list.append(gain_sum)
    return (jnp.stack(query_list), jnp.stack(trunk_sums).astype(jnp.bfloat16), jnp.stack(gain_list))
```

```python
import functools
import math

import jax
import jax.numpy as jnp
from jax import lax
from jax.experimental import pallas as pl
from jax.experimental.pallas import tpu as pltpu
from jax.sharding import PartitionSpec as P

QH = 20
KVH = 4
GROUP = 5
HD = 128
ROWS = 128
EPSILON = 1e-05
SCALE = 1.0 / math.sqrt(HD)
EXP_SCALE = SCALE * math.log2(math.e)
NZ = 8
BLOCK = 4 * ROWS
D = 5120
QUARTER = D // 4
W_ROWS = 160
bf16 = jnp.bfloat16
f32 = jnp.float32

SMEM = pl.BlockSpec(memory_space=pltpu.SMEM)
VMEM = pl.BlockSpec(memory_space=pltpu.VMEM)
ANY = pl.BlockSpec(memory_space=pl.ANY)
NT = (((1,), (1,)), ((), ()))
TN = (((0,), (0,)), ((), ()))


def call(body, out_shape, in_specs, flops, nbytes, scratch=(), aliases=None, exps=0):
    return pl.pallas_call(
        body,
        out_shape=out_shape,
        in_specs=in_specs,
        out_specs=[VMEM] * len(out_shape),
        scratch_shapes=list(scratch),
        input_output_aliases=aliases or {},
        compiler_params=pltpu.CompilerParams(vmem_limit_bytes=40 * 1024 * 1024),
        cost_estimate=pl.CostEstimate(flops=flops, bytes_accessed=nbytes, transcendentals=exps),
    )


def sds(shape, dtype):
    return jax.ShapeDtypeStruct(shape, dtype)


def split_kv_body(info, k, v, *outs):
    i = info[1]
    for p in range(4):
        cols = pl.ds(pl.multiple_of((i ^ p) * HD, HD), HD)
        outs[p][...] = k[:, cols]
        outs[4 + p][...] = v[:, cols]


def split_q_body(info, q, g, o, *outs):
    i = info[1]
    width = GROUP * HD
    for p in range(4):
        start = pl.multiple_of((i ^ p) * width, HD)
        cols = pl.ds(start, width)
        outs[p][...] = q[:, cols]
        outs[4 + p][...] = g[:, cols]
        rows = []
        for h in range(GROUP):
            head = pl.ds(pl.multiple_of(start + h * HD, HD), HD)
            product = g[:, head].astype(f32) * o[:, head].astype(f32)
            rows.append(jnp.sum(product.T, axis=0, keepdims=True))
        rows.append(jnp.zeros((8 - GROUP, ROWS), f32))
        outs[8 + p][...] = jnp.concatenate(rows, axis=0)


def head_rows(pieces, h):
    cols = pl.ds(pl.multiple_of(h * HD, HD), HD)
    return jnp.concatenate([piece[:, cols] for piece in pieces], axis=0)


def causal_mask(i):
    row = lax.broadcasted_iota(jnp.int32, (BLOCK, BLOCK), 0)
    col = lax.broadcasted_iota(jnp.int32, (BLOCK, BLOCK), 1)
    key_pos = (row ^ (i * ROWS))
    query_pos = (col ^ (i * ROWS))
    return key_pos <= query_pos


def stats_body(js, first, last, info, *refs):
    z, i = info[0], info[1]
    q = refs[:4]
    keys = refs[4 : 4 + len(js)]
    rest = refs[4 + len(js) :]
    if first:
        m_ref, l_ref = rest
        m_ref[...] = jnp.full(m_ref.shape, -1e30, f32)
        l_ref[...] = jnp.zeros(l_ref.shape, f32)
    else:
        m_in, l_in, m_ref, l_ref = rest
        m_ref[...] = m_in[...]
        l_ref[...] = l_in[...]
    for j, key in zip(js, keys):

        @pl.when(j <= z)
        def _(j=j, key=key):
            @pl.loop(0, GROUP)
            def _(h):
                scores = lax.dot_general(key[...], head_rows(q, h), NT, preferred_element_type=f32)
                if j == 0:
                    scores = jnp.where(causal_mask(i), scores, -1e30)
                row = pl.ds(h, 1)
                m_old = m_ref[row, :]
                m_new = jnp.maximum(m_old, jnp.max(scores, axis=0, keepdims=True))
                shift = m_new * EXP_SCALE
                total = jnp.sum(jnp.exp2(scores * EXP_SCALE - shift), axis=0, keepdims=True)
                l_ref[row, :] = l_ref[row, :] * jnp.exp2(m_old * EXP_SCALE - shift) + total
                m_ref[row, :] = m_new

    if last:
        l_ref[...] = jnp.where(l_ref[...] > 0.0, l_ref[...], 1.0)
        m_ref[...] = m_ref[...] * EXP_SCALE + jnp.log2(l_ref[...])


def grads_body(js, first, last, info, *refs):
    z, i = info[0], info[1]
    n = len(js)
    q, g = refs[:4], refs[4:8]
    shift_ref, delta_ref = refs[8:10]
    keys = refs[10 : 10 + n]
    values = refs[10 + n : 10 + 2 * n]
    rest = refs[10 + 2 * n :]
    if not first:
        dq_in, rest = rest[0], rest[1:]
    outs = rest[:n]
    rest = rest[n:]
    if last:
        dq_outs, rest = rest[:4], rest[4:]
        dq, dk, dv = rest
        dq[...] = dq_in[...]
    else:
        dq, dk, dv = rest
        if first:
            dq[...] = jnp.zeros(dq.shape, f32)
        else:
            dq[...] = dq_in[...]
    for j, key, value, out in zip(js, keys, values, outs):

        @pl.when(j <= z)
        def _(j=j, key=key, value=value, out=out):
            dk[...] = jnp.zeros(dk.shape, f32)
            dv[...] = jnp.zeros(dv.shape, f32)

            @pl.loop(0, GROUP)
            def _(h):
                qh = head_rows(q, h)
                gh = head_rows(g, h)
                row = pl.ds(h, 1)
                scores = lax.dot_general(key[...], qh, NT, preferred_element_type=f32)
                probs = jnp.exp2(scores * EXP_SCALE - shift_ref[row, :])
                if j == 0:
                    probs = jnp.where(causal_mask(i), probs, 0.0)
                dprobs = lax.dot_general(value[...], gh, NT, preferred_element_type=f32)
                dscores = (probs * (dprobs - delta_ref[row, :])).astype(bf16)
                dv[...] += jnp.dot(probs.astype(bf16), gh, preferred_element_type=f32)
                dk[...] += jnp.dot(dscores, qh, preferred_element_type=f32)
                dq[h] += lax.dot_general(dscores, key[...], TN, preferred_element_type=f32)

            out[:, :HD] = (dk[...] * SCALE).astype(bf16)
            out[:, HD:] = dv[...].astype(bf16)

        @pl.when(j > z)
        def _(out=out):
            out[...] = jnp.zeros(out.shape, bf16)

    if last:
        for p in range(4):
            for h in range(GROUP):
                dq_outs[p][:, h * HD : (h + 1) * HD] = (
                    dq[h, p * ROWS : (p + 1) * ROWS, :] * SCALE
                ).astype(bf16)


def join_q_body(info, *refs):
    i = info[1]
    width = GROUP * HD
    for p in range(4):
        refs[4][:, pl.ds(pl.multiple_of((i ^ p) * width, HD), width)] = refs[p][...]


def final_body(info, *refs):
    z, i, y = info[0], info[1], info[2]
    pieces = refs[:4]
    trunk, gains = refs[4:6]
    weights = refs[6 : 6 + 2 * NZ]
    outs = refs[6 + 2 * NZ : 10 + 2 * NZ]
    gain_out = refs[10 + 2 * NZ]
    whole, proj, left, sems = refs[11 + 2 * NZ :]
    copies = []
    for j in range(NZ):
        other = lax.rem(z - j + NZ, NZ)
        for c in range(2):
            for x in range(2):
                p = 2 * x + c
                start = pl.multiple_of((4 * other + (i ^ p)) * W_ROWS, 32)
                copy = pltpu.make_async_copy(
                    weights[2 * j + c].at[pl.ds(x * W_ROWS, W_ROWS), :],
                    whole.at[pl.ds(start, W_ROWS), :],
                    sems.at[4 * j + 2 * c + x],
                )
                copy.start()
                copies.append(copy)
    for p in range(4):
        head = i ^ p
        left[:, pl.ds(pl.multiple_of(head * HD, HD), HD)] = pieces[p][:, :HD]
        left[:, pl.ds(pl.multiple_of(KVH * HD + head * HD, HD), HD)] = pieces[p][:, HD:]
    squares = jnp.zeros((ROWS, 1), f32)
    for d in range(4):
        hidden = trunk[:, d * QUARTER : (d + 1) * QUARTER].astype(f32)
        squares = squares + jnp.sum(hidden * hidden, axis=1, keepdims=True)
    inverse = lax.rsqrt(squares * (1.0 / D) + EPSILON)
    for copy in copies:
        copy.wait()
    row_stat = jnp.zeros((ROWS, 1), f32)
    for d in range(4):
        cols = pl.ds(pl.multiple_of(lax.rem(y + d, 4) * QUARTER, QUARTER), QUARTER)
        part = lax.dot_general(left[...], whole[cols, :], NT, preferred_element_type=f32)
        normed = trunk[:, cols].astype(f32) * inverse
        product = part * normed
        gain_out[:, cols] = jnp.sum(product, axis=0, keepdims=True)
        row_stat = row_stat + jnp.sum(product * gains[:, cols], axis=1, keepdims=True)
        proj[d] = part
    row_stat = row_stat * (1.0 / D)
    for d in range(4):
        cols = pl.ds(pl.multiple_of(lax.rem(y + d, 4) * QUARTER, QUARTER), QUARTER)
        normed = trunk[:, cols].astype(f32) * inverse
        outs[d][...] = ((gains[:, cols] * proj[d] - normed * row_stat) * inverse).astype(bf16)


def seq_permute(x, pairs):
    return lax.ppermute(x, "seq", pairs)


def swap(x, p):
    return seq_permute(x, [(s, s ^ p) for s in range(4 * NZ)])


def shift(x, step, sources=range(NZ)):
    pairs = []
    for z in sources:
        z = z % NZ
        for i in range(4):
            pairs.append((4 * z + i, 4 * ((z + step) % NZ) + i))
    return seq_permute(x, pairs)


def ring_gather(x):
    blocks = {0: x}
    up = down = x
    for k in range(1, 5):
        up = shift(up, 1, range(k - 1, NZ - 1))
        blocks[k] = up
        if k < 4:
            down = shift(down, -1, [b - k + 1 for b in range(3)])
            blocks[NZ - k] = down
    return blocks


def add(a, b):
    return (a.astype(f32) + b.astype(f32)).astype(bf16)


def per_device(trunk, gains, queries, keys, values, outputs, out_grad, kv_weight):
    seq = lax.axis_index("seq")
    info = jnp.stack([seq // 4, seq % 4, lax.axis_index("head")]).astype(jnp.int32)
    piece = sds((ROWS, HD), bf16)
    kv = call(split_kv_body, [piece] * 8, [SMEM, VMEM, VMEM], 0, 1 << 19)(
        info, keys[0, 0], values[0, 0]
    )
    k_own = jnp.concatenate([kv[0]] + [swap(kv[p], p) for p in (1, 2, 3)], axis=0)
    v_own = jnp.concatenate([kv[4]] + [swap(kv[4 + p], p) for p in (1, 2, 3)], axis=0)
    wide = sds((ROWS, GROUP * HD), bf16)
    small = sds((8, ROWS), f32)
    qg = call(split_q_body, [wide] * 8 + [small] * 4, [SMEM, VMEM, VMEM, VMEM], 0, 1 << 22)(
        info, queries[0, 0], out_grad[0, 0], outputs[0, 0]
    )
    q = [qg[0]] + [swap(qg[p], p) for p in (1, 2, 3)]
    g = [qg[4]] + [swap(qg[4 + p], p) for p in (1, 2, 3)]
    delta = jnp.concatenate([qg[8]] + [swap(qg[8 + p], p) for p in (1, 2, 3)], axis=1)
    k_blocks = ring_gather(k_own)
    v_blocks = ring_gather(v_own)

    weight = kv_weight[0]
    pair = jnp.concatenate([weight, swap(weight, 2)], axis=0)
    w_blocks = {0: pair}
    up = down = pair
    for k in range(1, 5):
        up = shift(up, 1)
        w_blocks[k] = up
        if k < 4:
            down = shift(down, -1)
            w_blocks[NZ - k] = down
    w_list = []
    for j in range(NZ):
        w_list += [w_blocks[j], swap(w_blocks[j], 1)]

    unit = BLOCK * BLOCK * GROUP
    stat = sds((8, BLOCK), f32)
    carry = ()
    groups = [(0,), (1, 7), (2, 6), (3, 5, 4)]
    for n, js in enumerate(groups):
        carry = call(
            functools.partial(stats_body, js, n == 0, n == len(groups) - 1),
            [stat, stat],
            [SMEM] + [VMEM] * (4 + len(js) + len(carry)),
            2 * unit * HD * len(js),
            1 << 20,
            exps=unit * len(js),
        )(info, *q, *[k_blocks[j] for j in js], *carry)
    row_shift = carry[0]

    groups = [(4, 5), (3, 6), (2, 7), (1, 0)]
    dq_shape = sds((GROUP, BLOCK, HD), f32)
    pair_shape = sds((BLOCK, 2 * HD), bf16)
    acc = pltpu.VMEM((BLOCK, HD), f32)
    dq = ()
    terms = {}
    for n, js in enumerate(groups):
        first, last = n == 0, n == len(groups) - 1
        outs = [pair_shape] * len(js) + ([wide] * 4 if last else [dq_shape])
        res = call(
            functools.partial(grads_body, js, first, last),
            outs,
            [SMEM] + [VMEM] * (10 + 2 * len(js) + len(dq)),
            10 * unit * HD * len(js),
            4 << 20,
            scratch=([pltpu.VMEM((GROUP, BLOCK, HD), f32)] if last else []) + [acc, acc],
            exps=unit * len(js),
        )(
            info, *q, *g, row_shift, delta,
            *[k_blocks[j] for j in js], *[v_blocks[j] for j in js], *dq,
        )
        for j, term in zip(js, res):
            terms[j] = term
        dq = tuple(res[len(js) :])
    right = terms[4]
    left = terms[5]
    for k in (4, 3, 2):
        right = add(shift(right, -1, range(k, NZ)), terms[k - 1])
        left = shift(left, 1, [b + 9 - k for b in range(3)])
        if k > 2:
            left = add(left, terms[10 - k])
    right = shift(right, -1, range(1, NZ))
    kv_rows = (terms[0].astype(f32) + right.astype(f32) + left.astype(f32)).astype(bf16)
    kv_parts = [kv_rows[p * ROWS : (p + 1) * ROWS] for p in range(4)]
    kv_parts = [kv_parts[0]] + [swap(kv_parts[p], p) for p in (1, 2, 3)]

    query_grad = call(
        join_q_body, [sds((ROWS, QH * HD), bf16)], [SMEM] + [VMEM] * 4, 0, 1 << 20
    )(info, dq[0], *[swap(dq[p], p) for p in (1, 2, 3)])[0]

    quarter = sds((ROWS, QUARTER), bf16)
    res = call(
        final_body,
        [quarter] * 4 + [sds((1, D), f32)],
        [SMEM] + [VMEM] * 6 + [ANY] * (2 * NZ),
        2 * ROWS * D * 1024,
        12 << 20,
        scratch=[
            pltpu.VMEM((D, 2 * KVH * HD), bf16),
            pltpu.VMEM((4, ROWS, QUARTER), f32),
            pltpu.VMEM((ROWS, 2 * KVH * HD), bf16),
            pltpu.SemaphoreType.DMA((4 * NZ,)),
        ],
    )(info, *kv_parts, trunk[0], gains, *w_list)
    total = res[0].astype(f32)
    for d in (1, 2, 3):
        total = total + lax.ppermute(
            res[d], "head", [(y, (y + d) % 4) for y in range(4)]
        ).astype(f32)
    trunk_grad = total.astype(bf16)

    gain = res[4].reshape(D // 128, 128)
    gain = gain + swap(gain, 1)
    gain = gain + lax.ppermute(gain, "dp", [(0, 1), (1, 0)])
    for p in (2, 4, 8, 16):
        gain = gain + swap(gain, p)
    return (query_grad[None, None], trunk_grad[None], gain.reshape(1, D))


def solution(mesh):
    placed = (
        P("dp", "seq", None),
        P("head", None),
        P("head", "dp", "seq", None),
        P("head", "dp", "seq", None),
        P("head", "dp", "seq", None),
        P("head", "dp", "seq", None),
        P("head", "dp", "seq", None),
        P("head", "seq", None),
    )
    return jax.shard_map(
        per_device,
        mesh=mesh,
        in_specs=placed,
        out_specs=(P("head", "dp", "seq", None), P("dp", "seq", "head"), P("head", None)),
        check_vma=False,
    )
```

```python
import functools
import math

import jax
import jax.numpy as jnp
from jax import lax
from jax.experimental import pallas as pl
from jax.experimental.pallas import tpu as pltpu
from jax.sharding import PartitionSpec as P

QH = 20
KVH = 4
GROUP = 5
HD = 128
ROWS = 128
EPSILON = 1e-05
SCALE = 1.0 / math.sqrt(HD)
EXP_SCALE = SCALE * math.log2(math.e)
NZ = 8
BLOCK = 4 * ROWS
D = 5120
QUARTER = D // 4
WIDTH = GROUP * HD
G_WIDTH = WIDTH + HD
bf16 = jnp.bfloat16
f32 = jnp.float32

SMEM = pl.BlockSpec(memory_space=pltpu.SMEM)
VMEM = pl.BlockSpec(memory_space=pltpu.VMEM)
NT = (((1,), (1,)), ((), ()))
TN = (((0,), (0,)), ((), ()))


def call(body, out_shape, in_specs, flops, nbytes, scratch=(), aliases=None, exps=0):
    return pl.pallas_call(
        body,
        out_shape=out_shape,
        in_specs=in_specs,
        out_specs=[VMEM] * len(out_shape),
        scratch_shapes=list(scratch),
        input_output_aliases=aliases or {},
        compiler_params=pltpu.CompilerParams(vmem_limit_bytes=40 * 1024 * 1024),
        cost_estimate=pl.CostEstimate(flops=flops, bytes_accessed=nbytes, transcendentals=exps),
    )


def sds(shape, dtype):
    return jax.ShapeDtypeStruct(shape, dtype)


def split_kv_body(info, k, v, own, far, send):
    i = info[1]
    for p, (out, start) in enumerate(((own, 0), (send, 0), (far, 0), (send, 2 * HD))):
        cols = pl.ds(pl.multiple_of((i ^ p) * HD, HD), HD)
        out[:, start : start + HD] = k[:, cols]
        out[:, start + HD : start + 2 * HD] = v[:, cols]


def split_q_body(info, q, own, far, send):
    i = info[1]
    for p, (out, start) in enumerate(((own, 0), (send, 0), (far, 0), (send, WIDTH))):
        cols = pl.ds(pl.multiple_of((i ^ p) * WIDTH, HD), WIDTH)
        out[:, start : start + WIDTH] = q[:, cols]


def split_g_body(info, g, o, own, far, send):
    i = info[1]
    lane = lax.broadcasted_iota(jnp.int32, (ROWS, HD), 1)
    for p, (out, start) in enumerate(((own, 0), (send, 0), (far, 0), (send, G_WIDTH))):
        first = pl.multiple_of((i ^ p) * WIDTH, HD)
        out[:, start : start + WIDTH] = g[:, pl.ds(first, WIDTH)]
        coded = jnp.zeros((ROWS, HD), f32)
        for h in range(GROUP):
            head = pl.ds(pl.multiple_of(first + h * HD, HD), HD)
            product = g[:, head].astype(f32) * o[:, head].astype(f32)
            total = jnp.sum(product, axis=1, keepdims=True)
            for part in range(3):
                rounded = total.astype(bf16).astype(f32)
                coded = jnp.where(lane == 8 * part + h, rounded, coded)
                total = total - rounded
        out[:, start + WIDTH : start + G_WIDTH] = coded.astype(bf16)


def head_rows(pieces, h):
    cols = pl.ds(pl.multiple_of(h * HD, HD), HD)
    return jnp.concatenate([piece[:, cols] for piece in pieces], axis=0)


def causal_mask(i):
    row = lax.broadcasted_iota(jnp.int32, (BLOCK, BLOCK), 0)
    col = lax.broadcasted_iota(jnp.int32, (BLOCK, BLOCK), 1)
    key_pos = (row ^ (i * ROWS))
    query_pos = (col ^ (i * ROWS))
    return key_pos <= query_pos


def stats_body(js, first, last, info, *refs):
    z, i = info[0], info[1]
    q = refs[:3]
    if last:
        g = refs[3:6]
        refs = refs[3:]
    keys = refs[3 : 3 + len(js)]
    rest = refs[3 + len(js) :]
    if last:
        delta_ref = rest[-1]
        rest = rest[:-1]
    if first:
        m_ref, l_ref = rest
        m_ref[...] = jnp.full(m_ref.shape, -1e30, f32)
        l_ref[...] = jnp.zeros(l_ref.shape, f32)
    else:
        m_in, l_in, m_ref, l_ref = rest
        m_ref[...] = m_in[...]
        l_ref[...] = l_in[...]
    for j, key in zip(js, keys):

        @pl.when(j <= z)
        def _(j=j, key=key):
            @pl.loop(0, GROUP)
            def _(h):
                scores = lax.dot_general(key[:, :HD], head_rows(q, h), NT, preferred_element_type=f32)
                if j == 0:
                    scores = jnp.where(causal_mask(i), scores, -1e30)
                row = pl.ds(h, 1)
                m_old = m_ref[row, :]
                m_new = jnp.maximum(m_old, jnp.max(scores, axis=0, keepdims=True))
                shift = m_new * EXP_SCALE
                total = jnp.sum(jnp.exp2(scores * EXP_SCALE - shift), axis=0, keepdims=True)
                l_ref[row, :] = l_ref[row, :] * jnp.exp2(m_old * EXP_SCALE - shift) + total
                m_ref[row, :] = m_new

    if last:
        l_ref[...] = jnp.where(l_ref[...] > 0.0, l_ref[...], 1.0)
        m_ref[...] = m_ref[...] * EXP_SCALE + jnp.log2(l_ref[...])
        for p, (piece, start) in enumerate(((g[0], 0), (g[1], 0), (g[2], 0), (g[2], ROWS))):
            coded = piece[start : start + ROWS, WIDTH:G_WIDTH].astype(f32).T
            delta_ref[:, p * ROWS : (p + 1) * ROWS] = coded[:8] + coded[8:16] + coded[16:24]


def grads_body(js, first, last, info, *refs):
    z, i = info[0], info[1]
    n = len(js)
    q, g = refs[:3], refs[3:6]
    shift_ref, delta_ref = refs[6:8]
    blocks = refs[8 : 8 + n]
    rest = refs[8 + n :]
    if not first:
        dq_in, rest = rest[0], rest[1:]
    outs = rest[:n]
    rest = rest[n:]
    if last:
        dq_outs, rest = rest[:3], rest[3:]
        dq, dk, dv = rest
        dq[...] = dq_in[...]
    else:
        dq, dk, dv = rest
        if first:
            dq[...] = jnp.zeros(dq.shape, f32)
        else:
            dq[...] = dq_in[...]
    for j, block, out in zip(js, blocks, outs):

        @pl.when(j <= z)
        def _(j=j, block=block, out=out):
            key, value = block[:, :HD], block[:, HD:]
            dk[...] = jnp.zeros(dk.shape, f32)
            dv[...] = jnp.zeros(dv.shape, f32)

            @pl.loop(0, GROUP)
            def _(h):
                qh = head_rows(q, h)
                gh = head_rows(g, h)
                row = pl.ds(h, 1)
                scores = lax.dot_general(key, qh, NT, preferred_element_type=f32)
                probs = jnp.exp2(scores * EXP_SCALE - shift_ref[row, :])
                if j == 0:
                    probs = jnp.where(causal_mask(i), probs, 0.0)
                dprobs = lax.dot_general(value, gh, NT, preferred_element_type=f32)
                dscores = (probs * (dprobs - delta_ref[row, :])).astype(bf16)
                dv[...] += jnp.dot(probs.astype(bf16), gh, preferred_element_type=f32)
                dk[...] += jnp.dot(dscores, qh, preferred_element_type=f32)
                dq[h] += lax.dot_general(dscores, key, TN, preferred_element_type=f32)

            out[:, :HD] = (dk[...] * SCALE).astype(bf16)
            out[:, HD:] = dv[...].astype(bf16)

        @pl.when(j > z)
        def _(out=out):
            out[...] = jnp.zeros(out.shape, bf16)

    if last:
        for out, start in zip(dq_outs, (0, ROWS, 2 * ROWS)):
            for h in range(GROUP):
                rows = dq[h, start : start + out.shape[0], :]
                out[:, h * HD : (h + 1) * HD] = (rows * SCALE).astype(bf16)


def join_q_body(info, own, far, near, out):
    i = info[1]
    for p, (piece, start) in enumerate(((own, 0), (near, 0), (far, 0), (near, ROWS))):
        cols = pl.ds(pl.multiple_of((i ^ p) * WIDTH, HD), WIDTH)
        out[:, cols] = piece[start : start + ROWS, :]


def final_body(info, own, far, near, trunk, gains, whole, *refs):
    i, y = info[1], info[2]
    outs, (gain_out, proj, left) = refs[:4], refs[4:]
    for p, (piece, start) in enumerate(((own, 0), (near, 0), (far, 0), (near, ROWS))):
        head = i ^ p
        rows = slice(start, start + ROWS)
        left[:, pl.ds(pl.multiple_of(head * HD, HD), HD)] = piece[rows, :HD]
        left[:, pl.ds(pl.multiple_of(KVH * HD + head * HD, HD), HD)] = piece[rows, HD:]
    squares = jnp.zeros((ROWS, 1), f32)
    for d in range(4):
        hidden = trunk[:, d * QUARTER : (d + 1) * QUARTER].astype(f32)
        squares = squares + jnp.sum(hidden * hidden, axis=1, keepdims=True)
    inverse = lax.rsqrt(squares * (1.0 / D) + EPSILON)
    row_stat = jnp.zeros((ROWS, 1), f32)
    for d in range(4):
        cols = pl.ds(pl.multiple_of(lax.rem(y + d, 4) * QUARTER, QUARTER), QUARTER)
        part = lax.dot_general(left[...], whole[cols, :], NT, preferred_element_type=f32)
        normed = trunk[:, cols].astype(f32) * inverse
        product = part * normed
        gain_out[:, cols] = jnp.sum(product, axis=0, keepdims=True)
        row_stat = row_stat + jnp.sum(product * gains[:, cols], axis=1, keepdims=True)
        proj[d] = part
    row_stat = row_stat * (1.0 / D)
    for d in range(4):
        cols = pl.ds(pl.multiple_of(lax.rem(y + d, 4) * QUARTER, QUARTER), QUARTER)
        normed = trunk[:, cols].astype(f32) * inverse
        outs[d][...] = ((gains[:, cols] * proj[d] - normed * row_stat) * inverse).astype(bf16)


def seq_permute(x, pairs):
    return lax.ppermute(x, "seq", pairs)


def swap(x, p):
    return seq_permute(x, [(s, s ^ p) for s in range(4 * NZ)])


def shift(x, step, sources=range(NZ)):
    pairs = []
    for z in sources:
        z = z % NZ
        for i in range(4):
            pairs.append((4 * z + i, 4 * ((z + step) % NZ) + i))
    return seq_permute(x, pairs)


def ring_gather(x):
    blocks = {0: x}
    up = down = x
    for k in range(1, 5):
        up = shift(up, 1, range(k - 1, NZ - 1))
        blocks[k] = up
        if k < 4:
            down = shift(down, -1, [b - k + 1 for b in range(3)])
            blocks[NZ - k] = down
    return blocks


def parts_of(width):
    return [sds((ROWS, width), bf16), sds((ROWS, width), bf16), sds((ROWS, 2 * width), bf16)]


def rows_of(own, far, send, cut=True):
    width = own.shape[1]
    near = swap(send, 1)
    both = swap(jnp.concatenate([far, near[:, width:]], axis=0), 2)
    return [own, near[:, :width] if cut else near, both]


def rows_back(own, near, far):
    far = swap(far, 2)
    near = swap(jnp.concatenate([near, far[ROWS:]], axis=0), 1)
    return own, far, near


def add(a, b):
    return (a.astype(f32) + b.astype(f32)).astype(bf16)


def per_device(trunk, gains, queries, keys, values, outputs, out_grad, kv_weight):
    seq = lax.axis_index("seq")
    info = jnp.stack([seq // 4, seq % 4, lax.axis_index("head")]).astype(jnp.int32)
    whole = lax.all_gather(kv_weight[0], "seq", axis=0, tiled=True)
    own, far, send = call(split_kv_body, parts_of(2 * HD), [SMEM, VMEM, VMEM], 0, 1 << 19)(
        info, keys[0, 0], values[0, 0]
    )
    kv_own = jnp.concatenate(rows_of(own, far, send), axis=0)
    q = rows_of(
        *call(split_q_body, parts_of(WIDTH), [SMEM, VMEM], 0, 1 << 20)(info, queries[0, 0])
    )
    g = rows_of(
        *call(split_g_body, parts_of(G_WIDTH), [SMEM, VMEM, VMEM], 0, 1 << 21)(
            info, out_grad[0, 0], outputs[0, 0]
        ),
        cut=False,
    )
    blocks = ring_gather(kv_own)

    unit = BLOCK * BLOCK * GROUP
    stat = sds((8, BLOCK), f32)
    carry = ()
    groups = [(0,), (1, 7), (2, 6), (3, 5, 4)]
    for n, js in enumerate(groups):
        last = n == len(groups) - 1
        operands = [*q, *(g if last else []), *[blocks[j] for j in js], *carry]
        carry = call(
            functools.partial(stats_body, js, n == 0, last),
            [stat] * (3 if last else 2),
            [SMEM] + [VMEM] * len(operands),
            2 * unit * HD * len(js),
            1 << 20,
            exps=unit * len(js),
        )(info, *operands)
    row_shift, _, delta = carry

    groups = [(4, 5), (3, 6), (2, 7), (1, 0)]
    dq_shape = sds((GROUP, BLOCK, HD), f32)
    pair_shape = sds((BLOCK, 2 * HD), bf16)
    dq_parts = [sds((n, WIDTH), bf16) for n in (ROWS, ROWS, 2 * ROWS)]
    acc = pltpu.VMEM((BLOCK, HD), f32)
    dq = ()
    terms = {}
    for n, js in enumerate(groups):
        first, last = n == 0, n == len(groups) - 1
        outs = [pair_shape] * len(js) + (dq_parts if last else [dq_shape])
        operands = [*q, *g, row_shift, delta, *[blocks[j] for j in js], *dq]
        res = call(
            functools.partial(grads_body, js, first, last),
            outs,
            [SMEM] + [VMEM] * len(operands),
            10 * unit * HD * len(js),
            4 << 20,
            scratch=([pltpu.VMEM((GROUP, BLOCK, HD), f32)] if last else []) + [acc, acc],
            exps=unit * len(js),
        )(info, *operands)
        for j, term in zip(js, res):
            terms[j] = term
        dq = tuple(res[len(js) :])
    right = terms[4]
    left = terms[5]
    for k in (4, 3, 2):
        right = add(shift(right, -1, range(k, NZ)), terms[k - 1])
        left = shift(left, 1, [b + 9 - k for b in range(3)])
        if k > 2:
            left = add(left, terms[10 - k])
    right = shift(right, -1, range(1, NZ))
    kv_rows = (terms[0].astype(f32) + right.astype(f32) + left.astype(f32)).astype(bf16)
    kv_parts = rows_back(kv_rows, kv_rows[ROWS : 2 * ROWS], kv_rows[2 * ROWS :])

    query_grad = call(
        join_q_body, [sds((ROWS, QH * HD), bf16)], [SMEM] + [VMEM] * 3, 0, 1 << 20
    )(info, *rows_back(*dq))[0]
    trunk_rows, query_grad = lax.optimization_barrier((trunk[0], query_grad))

    quarter = sds((ROWS, QUARTER), bf16)
    res = call(
        final_body,
        [quarter] * 4 + [sds((1, D), f32)],
        [SMEM] + [VMEM] * 6,
        2 * ROWS * D * 1024,
        12 << 20,
        scratch=[
            pltpu.VMEM((4, ROWS, QUARTER), f32),
            pltpu.VMEM((ROWS, 2 * KVH * HD), bf16),
        ],
    )(info, *kv_parts, trunk_rows, gains, whole)
    total = res[0].astype(f32)
    for d in (1, 2, 3):
        total = total + lax.ppermute(
            res[d], "head", [(y, (y + d) % 4) for y in range(4)]
        ).astype(f32)
    trunk_grad = total.astype(bf16)

    gain = res[4].reshape(D // 128, 128)
    gain = gain + swap(gain, 1)
    gain = gain + lax.ppermute(gain, "dp", [(0, 1), (1, 0)])
    for p in (2, 4, 8, 16):
        gain = gain + swap(gain, p)
    return (query_grad[None, None], trunk_grad[None], gain.reshape(1, D))


def solution(mesh):
    placed = (
        P("dp", "seq", None),
        P("head", None),
        P("head", "dp", "seq", None),
        P("head", "dp", "seq", None),
        P("head", "dp", "seq", None),
        P("head", "dp", "seq", None),
        P("head", "dp", "seq", None),
        P("head", "seq", None),
    )
    return jax.shard_map(
        per_device,
        mesh=mesh,
        in_specs=placed,
        out_specs=(P("head", "dp", "seq", None), P("dp", "seq", "head"), P("head", None)),
        check_vma=False,
    )
```

```python
import functools
import math

import jax
import jax.numpy as jnp
from jax import lax
from jax.experimental import pallas as pl
from jax.experimental.pallas import tpu as pltpu
from jax.sharding import Mesh, PartitionSpec as P

QH = 20
KVH = 4
GROUP = 5
HD = 128
ROWS = 128
EPSILON = 1e-05
SCALE = 1.0 / math.sqrt(HD)
EXP_SCALE = SCALE * math.log2(math.e)
NZ = 8
BLOCK = 4 * ROWS
D = 5120
QUARTER = D // 4
TILE = 256
SEQ = ("z", "x_hi", "core")
WIDTH = GROUP * HD
G_WIDTH = WIDTH + HD
bf16 = jnp.bfloat16
f32 = jnp.float32

SMEM = pl.BlockSpec(memory_space=pltpu.SMEM)
VMEM = pl.BlockSpec(memory_space=pltpu.VMEM)
NT = (((1,), (1,)), ((), ()))
TN = (((0,), (0,)), ((), ()))


def call(body, out_shape, in_specs, flops, nbytes, scratch=(), exps=0, vmem=40):
    return pl.pallas_call(
        body,
        out_shape=out_shape,
        in_specs=in_specs,
        out_specs=[VMEM] * len(out_shape),
        scratch_shapes=list(scratch),
        compiler_params=pltpu.CompilerParams(vmem_limit_bytes=vmem * 1024 * 1024),
        cost_estimate=pl.CostEstimate(flops=flops, bytes_accessed=nbytes, transcendentals=exps),
    )


def sds(shape, dtype):
    return jax.ShapeDtypeStruct(shape, dtype)


def split_kv_body(info, k, v, own, far, send):
    i = info[1]
    for p, (out, start) in enumerate(((own, 0), (send, 0), (far, 0), (send, 2 * HD))):
        cols = pl.ds(pl.multiple_of((i ^ p) * HD, HD), HD)
        out[:, start : start + HD] = k[:, cols]
        out[:, start + HD : start + 2 * HD] = v[:, cols]


def split_q_body(info, q, own, far, send):
    i = info[1]
    for p, (out, start) in enumerate(((own, 0), (send, 0), (far, 0), (send, WIDTH))):
        cols = pl.ds(pl.multiple_of((i ^ p) * WIDTH, HD), WIDTH)
        out[:, start : start + WIDTH] = q[:, cols]


def split_g_body(info, g, o, own, far, send):
    i = info[1]
    lane = lax.broadcasted_iota(jnp.int32, (ROWS, HD), 1)
    for p, (out, start) in enumerate(((own, 0), (send, 0), (far, 0), (send, G_WIDTH))):
        first = pl.multiple_of((i ^ p) * WIDTH, HD)
        out[:, start : start + WIDTH] = g[:, pl.ds(first, WIDTH)]
        coded = jnp.zeros((ROWS, HD), f32)
        for h in range(GROUP):
            head = pl.ds(pl.multiple_of(first + h * HD, HD), HD)
            product = g[:, head].astype(f32) * o[:, head].astype(f32)
            total = jnp.sum(product, axis=1, keepdims=True)
            for part in range(3):
                rounded = total.astype(bf16).astype(f32)
                coded = jnp.where(lane == 8 * part + h, rounded, coded)
                total = total - rounded
        out[:, start + WIDTH : start + G_WIDTH] = coded.astype(bf16)


def head_rows(pieces, h):
    cols = pl.ds(pl.multiple_of(h * HD, HD), HD)
    return jnp.concatenate([piece[:, cols] for piece in pieces], axis=0)


def causal_mask(i, u, rows, t):
    row = lax.broadcasted_iota(jnp.int32, (rows, TILE), 0) + u
    col = lax.broadcasted_iota(jnp.int32, (rows, TILE), 1) + t
    key_pos = row ^ (i * ROWS)
    query_pos = col ^ (i * ROWS)
    return key_pos <= query_pos


def stats_body(js, first, last, info, *refs):
    z, i = info[0], info[1]
    q = refs[:3]
    if last:
        g = refs[3:6]
        refs = refs[3:]
    keys = refs[3 : 3 + len(js)]
    rest = refs[3 + len(js) :]
    if last:
        delta_ref = rest[-1]
        rest = rest[:-1]
    if first:
        m_ref, l_ref = rest
        m_ref[...] = jnp.full(m_ref.shape, -1e30, f32)
        l_ref[...] = jnp.zeros(l_ref.shape, f32)
    else:
        m_in, l_in, m_ref, l_ref = rest
        m_ref[...] = m_in[...]
        l_ref[...] = l_in[...]
    for j, key in zip(js, keys):

        @pl.when(j <= z)
        def _(j=j, key=key):
            for h in range(GROUP):
                for t in range(0, BLOCK, TILE):
                    heads = head_rows(q, h)[t : t + TILE]
                    cols = slice(t, t + TILE)
                    m, total = m_ref[h : h + 1, cols], l_ref[h : h + 1, cols]
                    for u in range(0, BLOCK, ROWS):
                        scores = lax.dot_general(
                            key[u : u + ROWS, :HD], heads, NT, preferred_element_type=f32
                        )
                        if j == 0:
                            scores = jnp.where(causal_mask(i, u, ROWS, t), scores, -1e30)
                        m_new = jnp.maximum(m, jnp.max(scores, axis=0, keepdims=True))
                        shift = m_new * EXP_SCALE
                        total = total * jnp.exp2(m * EXP_SCALE - shift) + jnp.sum(
                            jnp.exp2(scores * EXP_SCALE - shift), axis=0, keepdims=True
                        )
                        m = m_new
                    m_ref[h : h + 1, cols] = m
                    l_ref[h : h + 1, cols] = total

    if last:
        l_ref[...] = jnp.where(l_ref[...] > 0.0, l_ref[...], 1.0)
        m_ref[...] = m_ref[...] * EXP_SCALE + jnp.log2(l_ref[...])
        for p, (piece, start) in enumerate(((g[0], 0), (g[1], 0), (g[2], 0), (g[2], ROWS))):
            coded = piece[start : start + ROWS, WIDTH:G_WIDTH].astype(f32).T
            delta_ref[:, p * ROWS : (p + 1) * ROWS] = coded[:8] + coded[8:16] + coded[16:24]


def grads_body(js, first, last, info, *refs):
    z, i = info[0], info[1]
    n = len(js)
    q, g = refs[:3], refs[3:6]
    shift_ref, delta_ref = refs[6:8]
    blocks = refs[8 : 8 + n]
    rest = refs[8 + n :]
    if not first:
        dq_in, rest = rest[0], rest[1:]
    outs = rest[:n]
    rest = rest[n:]
    if last:
        dq_outs, rest = rest[:3], rest[3:]
        dq, dk, dv = rest
        dq[...] = dq_in[...]
    else:
        dq, dk, dv = rest
        if first:
            dq[...] = jnp.zeros(dq.shape, f32)
        else:
            dq[...] = dq_in[...]
    for j, block, out in zip(js, blocks, outs):

        @pl.when(j <= z)
        def _(j=j, block=block, out=out):
            key, value = block[:, :HD], block[:, HD:]
            dk[...] = jnp.zeros(dk.shape, f32)
            dv[...] = jnp.zeros(dv.shape, f32)
            for h in range(GROUP):
                qh = head_rows(q, h)
                gh = head_rows(g, h)
                for t in range(0, BLOCK, TILE):
                    cols = slice(t, t + TILE)
                    row = pl.ds(h, 1)
                    scores = lax.dot_general(key, qh[cols], NT, preferred_element_type=f32)
                    probs = jnp.exp2(scores * EXP_SCALE - shift_ref[row, cols])
                    if j == 0:
                        probs = jnp.where(causal_mask(i, 0, BLOCK, t), probs, 0.0)
                    dprobs = lax.dot_general(value, gh[cols], NT, preferred_element_type=f32)
                    dscores = (probs * (dprobs - delta_ref[row, cols])).astype(bf16)
                    dv_part = jnp.dot(probs.astype(bf16), gh[cols], preferred_element_type=f32)
                    dk_part = jnp.dot(dscores, qh[cols], preferred_element_type=f32)
                    dv[...] += dv_part
                    dk[...] += dk_part
                    dq[h, :, cols] += lax.dot_general(key, dscores, TN, preferred_element_type=f32)
            out[:, :HD] = (dk[...] * SCALE).astype(bf16)
            out[:, HD:] = dv[...].astype(bf16)

        @pl.when(j > z)
        def _(out=out):
            out[...] = jnp.zeros(out.shape, bf16)

    if last:
        for out, start in zip(dq_outs, (0, ROWS, 2 * ROWS)):
            for h in range(GROUP):
                rows = dq[h, :, start : start + out.shape[0]].T
                out[:, h * HD : (h + 1) * HD] = (rows * SCALE).astype(bf16)


def join_q_body(info, own, far, near, out):
    i = info[1]
    for p, (piece, start) in enumerate(((own, 0), (near, 0), (far, 0), (near, ROWS))):
        cols = pl.ds(pl.multiple_of((i ^ p) * WIDTH, HD), WIDTH)
        out[:, cols] = piece[start : start + ROWS, :]


def final_body(info, own, far, near, trunk, gains, whole, *refs):
    i, y = info[1], info[2]
    outs, (gain_out, proj, left) = refs[:4], refs[4:]
    for p, (piece, start) in enumerate(((own, 0), (near, 0), (far, 0), (near, ROWS))):
        head = i ^ p
        rows = slice(start, start + ROWS)
        left[:, pl.ds(pl.multiple_of(head * HD, HD), HD)] = piece[rows, :HD]
        left[:, pl.ds(pl.multiple_of(KVH * HD + head * HD, HD), HD)] = piece[rows, HD:]
    squares = jnp.zeros((ROWS, 1), f32)
    for d in range(4):
        hidden = trunk[:, d * QUARTER : (d + 1) * QUARTER].astype(f32)
        squares = squares + jnp.sum(hidden * hidden, axis=1, keepdims=True)
    inverse = lax.rsqrt(squares * (1.0 / D) + EPSILON)
    row_stat = jnp.zeros((ROWS, 1), f32)
    for d in range(4):
        cols = pl.ds(pl.multiple_of(lax.rem(y + d, 4) * QUARTER, QUARTER), QUARTER)
        part = lax.dot_general(left[...], whole[cols, :], NT, preferred_element_type=f32)
        normed = trunk[:, cols].astype(f32) * inverse
        product = part * normed
        gain_out[:, cols] = jnp.sum(product, axis=0, keepdims=True)
        row_stat = row_stat + jnp.sum(product * gains[:, cols], axis=1, keepdims=True)
        proj[d] = part
    row_stat = row_stat * (1.0 / D)
    for d in range(4):
        cols = pl.ds(pl.multiple_of(lax.rem(y + d, 4) * QUARTER, QUARTER), QUARTER)
        normed = trunk[:, cols].astype(f32) * inverse
        outs[d][...] = ((gains[:, cols] * proj[d] - normed * row_stat) * inverse).astype(bf16)


def seq_permute(x, pairs):
    return lax.ppermute(x, SEQ, pairs)


def swap(x, p):
    return seq_permute(x, [(s, s ^ p) for s in range(4 * NZ)])


def shift(x, step):
    return seq_permute(x, [(s, (s + 4 * step) % (4 * NZ)) for s in range(4 * NZ)])


def stats(js, info, q, blocks, carry, g=()):
    unit = BLOCK * BLOCK * GROUP * len(js)
    stat = sds((8, BLOCK), f32)
    operands = [*q, *g, *[blocks[j] for j in js], *carry]
    return call(
        functools.partial(stats_body, js, not carry, bool(g)),
        [stat] * (3 if g else 2),
        [SMEM] + [VMEM] * len(operands),
        2 * unit * HD,
        1 << 20,
        exps=unit,
    )(info, *operands)


def parts_of(width):
    return [sds((ROWS, width), bf16), sds((ROWS, width), bf16), sds((ROWS, 2 * width), bf16)]


def rows_of(own, far, send, cut=True):
    width = own.shape[1]
    near = swap(send, 1)
    both = swap(jnp.concatenate([far, near[:, width:]], axis=0), 2)
    return [own, near[:, :width] if cut else near, both]


def add(a, b):
    return (a.astype(f32) + b.astype(f32)).astype(bf16)


def per_device(trunk, gains, queries, keys, values, outputs, out_grad, kv_weight):
    seq = lax.axis_index(SEQ)
    info = jnp.stack([seq // 4, seq % 4, lax.axis_index("head")]).astype(jnp.int32)
    whole = lax.all_gather(kv_weight[0], SEQ, axis=0, tiled=True)
    own, far, send = call(split_kv_body, parts_of(2 * HD), [SMEM, VMEM, VMEM], 0, 1 << 19)(
        info, keys[0, 0], values[0, 0]
    )
    near = swap(send, 1)
    near, query_rows, grad_rows = lax.optimization_barrier((near, queries[0, 0], out_grad[0, 0]))
    both = swap(jnp.concatenate([far, near[:, 2 * HD :]], axis=0), 2)
    kv_own = jnp.concatenate([own, near[:, : 2 * HD], both], axis=0)
    q_cut = call(split_q_body, parts_of(WIDTH), [SMEM, VMEM], 0, 1 << 20)(info, query_rows)
    g_cut = call(split_g_body, parts_of(G_WIDTH), [SMEM, VMEM, VMEM], 0, 1 << 21)(
        info, grad_rows, outputs[0, 0]
    )
    q = rows_of(*q_cut)
    g = rows_of(*g_cut, cut=False)
    blocks = {0: kv_own}
    up = down = kv_own
    carry = ()
    groups = {1: (0,), 2: (1, 7), 3: (2, 6), 4: (3, 5)}
    for k in range(1, 5):
        up = shift(up, 1)
        blocks[k] = up
        if k < 4:
            down = shift(down, -1)
            blocks[NZ - k] = down
        carry = stats(groups[k], info, q, blocks, carry)
        if k == 1:
            up, down, q = lax.optimization_barrier((up, down, q))
        elif k == 2:
            up, down, g, carry = lax.optimization_barrier((up, down, g, carry))
        elif k == 3:
            up, carry = lax.optimization_barrier((up, carry))
        if k < 4:
            blocks[k], blocks[NZ - k] = up, down
    row_shift, _, delta = stats((4,), info, q, blocks, carry, g)

    unit = BLOCK * BLOCK * GROUP
    groups = [(4, 5), (3, 6), (2, 7), (1, 0)]
    dq_shape = sds((GROUP, HD, BLOCK), f32)
    pair_shape = sds((BLOCK, 2 * HD), bf16)
    dq_parts = [sds((n, WIDTH), bf16) for n in (ROWS, ROWS, 2 * ROWS)]
    acc = pltpu.VMEM((BLOCK, HD), f32)
    dq = ()
    terms = {}
    for n, js in enumerate(groups):
        first, last = n == 0, n == len(groups) - 1
        outs = [pair_shape] * len(js) + (dq_parts if last else [dq_shape])
        operands = [*q, *g, row_shift, delta, *[blocks[j] for j in js], *dq]
        res = call(
            functools.partial(grads_body, js, first, last),
            outs,
            [SMEM] + [VMEM] * len(operands),
            10 * unit * HD * len(js),
            4 << 20,
            scratch=([pltpu.VMEM((GROUP, HD, BLOCK), f32)] if last else []) + [acc, acc],
            exps=unit * len(js),
        )(info, *operands)
        for j, term in zip(js, res):
            terms[j] = term
        dq = tuple(res[len(js) :])
    right = terms[4]
    left = terms[5]
    for k in (4, 3, 2):
        right = add(shift(right, -1), terms[k - 1])
        left = shift(left, 1)
        if k > 2:
            left = add(left, terms[10 - k])
    right = shift(right, -1)
    kv_rows = (terms[0].astype(f32) + right.astype(f32) + left.astype(f32)).astype(bf16)
    kv_rows, whole = lax.optimization_barrier((kv_rows, whole))
    kv_far = swap(kv_rows[2 * ROWS :], 2)
    kv_far, dq_send = lax.optimization_barrier((kv_far, dq[2]))
    kv_near = swap(jnp.concatenate([kv_rows[ROWS : 2 * ROWS], kv_far[ROWS:]], axis=0), 1)
    dq_far = swap(dq_send, 2)

    quarter = sds((ROWS, QUARTER), bf16)
    res = call(
        final_body,
        [quarter] * 4 + [sds((1, D), f32)],
        [SMEM] + [VMEM] * 6,
        2 * ROWS * D * 1024,
        12 << 20,
        scratch=[
            pltpu.VMEM((4, ROWS, QUARTER), f32),
            pltpu.VMEM((ROWS, 2 * KVH * HD), bf16),
        ],
        vmem=24,
    )(info, kv_rows, kv_far, kv_near, trunk[0], gains, whole)
    total = res[0].astype(f32)
    for d in (1, 2, 3):
        total = total + lax.ppermute(
            res[d], "head", [(y, (y + d) % 4) for y in range(4)]
        ).astype(f32)
    trunk_grad = total.astype(bf16)

    gain = res[4].reshape(D // HD, HD)
    for axes, n in ((("x_hi", "core", "dp"), 8), ("z", NZ)):
        spread = jnp.broadcast_to(gain[None], (n, D // HD, HD))
        gain = jnp.sum(lax.all_to_all(spread, axes, 0, 0, tiled=True), axis=0)
    dq_near = swap(jnp.concatenate([dq[1], dq_far[ROWS:]], axis=0), 1)
    query_grad = call(
        join_q_body, [sds((ROWS, QH * HD), bf16)], [SMEM] + [VMEM] * 3, 0, 1 << 20
    )(info, dq[0], dq_far, dq_near)[0]
    return (query_grad[None, None], trunk_grad[None], gain.reshape(1, D))


def solution(mesh):
    cut = Mesh(
        mesh.devices.reshape(4, NZ, 2, 2, 2), ("head",) + SEQ + ("dp",)
    )
    placed = (
        P("dp", SEQ, None),
        P("head", None),
        P("head", "dp", SEQ, None),
        P("head", "dp", SEQ, None),
        P("head", "dp", SEQ, None),
        P("head", "dp", SEQ, None),
        P("head", "dp", SEQ, None),
        P("head", SEQ, None),
    )
    return jax.shard_map(
        per_device,
        mesh=cut,
        in_specs=placed,
        out_specs=(P("head", "dp", SEQ, None), P("dp", SEQ, "head"), P("head", None)),
        check_vma=False,
    )
```

```python
import functools
import math

import jax
import jax.numpy as jnp
from jax import lax
from jax.experimental import pallas as pl
from jax.experimental.pallas import tpu as pltpu
from jax.sharding import Mesh, PartitionSpec as P

QH = 20
KVH = 4
GROUP = 5
HD = 128
ROWS = 128
EPSILON = 1e-05
SCALE = 1.0 / math.sqrt(HD)
EXP_SCALE = SCALE * math.log2(math.e)
NZ = 8
BLOCK = 4 * ROWS
D = 5120
QUARTER = D // 4
HALF = 80
TILE = 256
SEQ = ("z", "x_hi", "core")
WIDTH = GROUP * HD
G_WIDTH = WIDTH + HD
bf16 = jnp.bfloat16
f32 = jnp.float32

SMEM = pl.BlockSpec(memory_space=pltpu.SMEM)
VMEM = pl.BlockSpec(memory_space=pltpu.VMEM)
ANY = pl.BlockSpec(memory_space=pl.ANY)
NT = (((1,), (1,)), ((), ()))
TN = (((0,), (0,)), ((), ()))


def call(body, out_shape, in_specs, flops, nbytes, scratch=(), exps=0, vmem=40):
    return pl.pallas_call(
        body,
        out_shape=out_shape,
        in_specs=in_specs,
        out_specs=[VMEM] * len(out_shape),
        scratch_shapes=list(scratch),
        compiler_params=pltpu.CompilerParams(vmem_limit_bytes=vmem * 1024 * 1024),
        cost_estimate=pl.CostEstimate(flops=flops, bytes_accessed=nbytes, transcendentals=exps),
    )


def sds(shape, dtype):
    return jax.ShapeDtypeStruct(shape, dtype)


def split_kv_body(info, k, v, own, far, send):
    i = info[1]
    for p, (out, start) in enumerate(((own, 0), (send, 0), (far, 0), (send, 2 * HD))):
        cols = pl.ds(pl.multiple_of((i ^ p) * HD, HD), HD)
        out[:, start : start + HD] = k[:, cols]
        out[:, start + HD : start + 2 * HD] = v[:, cols]


def split_q_body(info, q, own, far, send):
    i = info[1]
    for p, (out, start) in enumerate(((own, 0), (send, 0), (far, 0), (send, WIDTH))):
        cols = pl.ds(pl.multiple_of((i ^ p) * WIDTH, HD), WIDTH)
        out[:, start : start + WIDTH] = q[:, cols]


def split_g_body(info, g, o, own, far, send):
    i = info[1]
    lane = lax.broadcasted_iota(jnp.int32, (ROWS, HD), 1)
    for p, (out, start) in enumerate(((own, 0), (send, 0), (far, 0), (send, G_WIDTH))):
        first = pl.multiple_of((i ^ p) * WIDTH, HD)
        out[:, start : start + WIDTH] = g[:, pl.ds(first, WIDTH)]
        coded = jnp.zeros((ROWS, HD), f32)
        for h in range(GROUP):
            head = pl.ds(pl.multiple_of(first + h * HD, HD), HD)
            product = g[:, head].astype(f32) * o[:, head].astype(f32)
            total = jnp.sum(product, axis=1, keepdims=True)
            for part in range(3):
                rounded = total.astype(bf16).astype(f32)
                coded = jnp.where(lane == 8 * part + h, rounded, coded)
                total = total - rounded
        out[:, start + WIDTH : start + G_WIDTH] = coded.astype(bf16)


def head_rows(pieces, h):
    cols = pl.ds(pl.multiple_of(h * HD, HD), HD)
    return jnp.concatenate([piece[:, cols] for piece in pieces], axis=0)


def causal_mask(i, u, rows, t):
    row = lax.broadcasted_iota(jnp.int32, (rows, TILE), 0) + u
    col = lax.broadcasted_iota(jnp.int32, (rows, TILE), 1) + t
    key_pos = row ^ (i * ROWS)
    query_pos = col ^ (i * ROWS)
    return key_pos <= query_pos


def stats_body(js, first, last, info, *refs):
    z, i = info[0], info[1]
    q = refs[:3]
    if last:
        g = refs[3:6]
        refs = refs[3:]
    keys = refs[3 : 3 + len(js)]
    rest = refs[3 + len(js) :]
    if last:
        delta_ref = rest[-1]
        rest = rest[:-1]
    if first:
        m_ref, l_ref = rest
        m_ref[...] = jnp.full(m_ref.shape, -1e30, f32)
        l_ref[...] = jnp.zeros(l_ref.shape, f32)
    else:
        m_in, l_in, m_ref, l_ref = rest
        m_ref[...] = m_in[...]
        l_ref[...] = l_in[...]
    for j, key in zip(js, keys):

        @pl.when(j <= z)
        def _(j=j, key=key):
            for h in range(GROUP):
                for t in range(0, BLOCK, TILE):
                    heads = head_rows(q, h)[t : t + TILE]
                    cols = slice(t, t + TILE)
                    m, total = m_ref[h : h + 1, cols], l_ref[h : h + 1, cols]
                    for u in range(0, BLOCK, ROWS):
                        scores = lax.dot_general(
                            key[u : u + ROWS, :HD], heads, NT, preferred_element_type=f32
                        )
                        if j == 0:
                            scores = jnp.where(causal_mask(i, u, ROWS, t), scores, -1e30)
                        m_new = jnp.maximum(m, jnp.max(scores, axis=0, keepdims=True))
                        shift = m_new * EXP_SCALE
                        total = total * jnp.exp2(m * EXP_SCALE - shift) + jnp.sum(
                            jnp.exp2(scores * EXP_SCALE - shift), axis=0, keepdims=True
                        )
                        m = m_new
                    m_ref[h : h + 1, cols] = m
                    l_ref[h : h + 1, cols] = total

    if last:
        l_ref[...] = jnp.where(l_ref[...] > 0.0, l_ref[...], 1.0)
        m_ref[...] = m_ref[...] * EXP_SCALE + jnp.log2(l_ref[...])
        for p, (piece, start) in enumerate(((g[0], 0), (g[1], 0), (g[2], 0), (g[2], ROWS))):
            coded = piece[start : start + ROWS, WIDTH:G_WIDTH].astype(f32).T
            delta_ref[:, p * ROWS : (p + 1) * ROWS] = coded[:8] + coded[8:16] + coded[16:24]


def grads_body(js, first, last, info, *refs):
    z, i = info[0], info[1]
    n = len(js)
    q, g = refs[:3], refs[3:6]
    shift_ref, delta_ref = refs[6:8]
    blocks = refs[8 : 8 + n]
    rest = refs[8 + n :]
    if not first:
        dq_in, rest = rest[0], rest[1:]
    outs = rest[:n]
    rest = rest[n:]
    if last:
        dq_outs, rest = rest[:3], rest[3:]
        dq, dk, dv = rest
        dq[...] = dq_in[...]
    else:
        dq, dk, dv = rest
        if first:
            dq[...] = jnp.zeros(dq.shape, f32)
        else:
            dq[...] = dq_in[...]
    for j, block, out in zip(js, blocks, outs):

        @pl.when(j <= z)
        def _(j=j, block=block, out=out):
            key, value = block[:, :HD], block[:, HD:]
            dk[...] = jnp.zeros(dk.shape, f32)
            dv[...] = jnp.zeros(dv.shape, f32)
            for h in range(GROUP):
                qh = head_rows(q, h)
                gh = head_rows(g, h)
                for t in range(0, BLOCK, TILE):
                    cols = slice(t, t + TILE)
                    row = pl.ds(h, 1)
                    scores = lax.dot_general(key, qh[cols], NT, preferred_element_type=f32)
                    probs = jnp.exp2(scores * EXP_SCALE - shift_ref[row, cols])
                    if j == 0:
                        probs = jnp.where(causal_mask(i, 0, BLOCK, t), probs, 0.0)
                    dprobs = lax.dot_general(value, gh[cols], NT, preferred_element_type=f32)
                    dscores = (probs * (dprobs - delta_ref[row, cols])).astype(bf16)
                    dv_part = jnp.dot(probs.astype(bf16), gh[cols], preferred_element_type=f32)
                    dk_part = jnp.dot(dscores, qh[cols], preferred_element_type=f32)
                    dv[...] += dv_part
                    dk[...] += dk_part
                    dq[h, :, cols] += lax.dot_general(key, dscores, TN, preferred_element_type=f32)
            out[:, :HD] = (dk[...] * SCALE).astype(bf16)
            out[:, HD:] = dv[...].astype(bf16)

        @pl.when(j > z)
        def _(out=out):
            out[...] = jnp.zeros(out.shape, bf16)

    if last:
        for out, start in zip(dq_outs, (0, ROWS, 2 * ROWS)):
            for h in range(GROUP):
                rows = dq[h, :, start : start + out.shape[0]].T
                out[:, h * HD : (h + 1) * HD] = (rows * SCALE).astype(bf16)


def join_q_body(info, own, far, near, out):
    i = info[1]
    for p, (piece, start) in enumerate(((own, 0), (near, 0), (far, 0), (near, ROWS))):
        cols = pl.ds(pl.multiple_of((i ^ p) * WIDTH, HD), WIDTH)
        out[:, cols] = piece[start : start + ROWS, :]


def join_weight_body(info, *refs):
    i, dp = info[1], info[3]
    whole, sems = refs[8:]
    copies = []
    for n in range(8):
        x = lax.rem(i // 2 * 2 + dp + n % 4, 4)
        block = x // 2 * 2 + (i % 2 if n < 4 else 1 - i % 2)
        place = pl.ds(pl.multiple_of(x % 2 * HALF, 16), HALF)
        copies.append(
            pltpu.make_async_copy(refs[n], whole.at[:, block, place, :], sems.at[n])
        )
        copies[n].start()
    for copy in copies:
        copy.wait()


def final_body(info, own, far, near, trunk, gains, whole, *refs):
    i, y = info[1], info[2]
    outs, (gain_out, proj, left) = refs[:4], refs[4:]
    for p, (piece, start) in enumerate(((own, 0), (near, 0), (far, 0), (near, ROWS))):
        head = i ^ p
        rows = slice(start, start + ROWS)
        left[:, pl.ds(pl.multiple_of(head * HD, HD), HD)] = piece[rows, :HD]
        left[:, pl.ds(pl.multiple_of(KVH * HD + head * HD, HD), HD)] = piece[rows, HD:]
    squares = jnp.zeros((ROWS, 1), f32)
    for d in range(4):
        hidden = trunk[:, d * QUARTER : (d + 1) * QUARTER].astype(f32)
        squares = squares + jnp.sum(hidden * hidden, axis=1, keepdims=True)
    inverse = lax.rsqrt(squares * (1.0 / D) + EPSILON)
    row_stat = jnp.zeros((ROWS, 1), f32)
    for d in range(4):
        cols = pl.ds(pl.multiple_of(lax.rem(y + d, 4) * QUARTER, QUARTER), QUARTER)
        weight = whole[pl.ds(2 * lax.rem(y + d, 4), 2)].reshape(QUARTER, 2 * KVH * HD)
        part = lax.dot_general(left[...], weight, NT, preferred_element_type=f32)
        normed = trunk[:, cols].astype(f32) * inverse
        product = part * normed
        gain_out[:, cols] = jnp.sum(product, axis=0, keepdims=True)
        row_stat = row_stat + jnp.sum(product * gains[:, cols], axis=1, keepdims=True)
        proj[d] = part
    row_stat = row_stat * (1.0 / D)
    for d in range(4):
        cols = pl.ds(pl.multiple_of(lax.rem(y + d, 4) * QUARTER, QUARTER), QUARTER)
        normed = trunk[:, cols].astype(f32) * inverse
        outs[d][...] = ((gains[:, cols] * proj[d] - normed * row_stat) * inverse).astype(bf16)


def seq_permute(x, pairs):
    return lax.ppermute(x, SEQ, pairs)


def swap(x, p):
    return seq_permute(x, [(s, s ^ p) for s in range(4 * NZ)])


def shift(x, step):
    return seq_permute(x, [(s, (s + 4 * step) % (4 * NZ)) for s in range(4 * NZ)])


def stats(js, info, q, blocks, carry, g=()):
    unit = BLOCK * BLOCK * GROUP * len(js)
    stat = sds((8, BLOCK), f32)
    operands = [*q, *g, *[blocks[j] for j in js], *carry]
    return call(
        functools.partial(stats_body, js, not carry, bool(g)),
        [stat] * (3 if g else 2),
        [SMEM] + [VMEM] * len(operands),
        2 * unit * HD,
        1 << 20,
        exps=unit,
    )(info, *operands)


def parts_of(width):
    return [sds((ROWS, width), bf16), sds((ROWS, width), bf16), sds((ROWS, 2 * width), bf16)]


def rows_of(own, far, send, cut=True):
    width = own.shape[1]
    near = swap(send, 1)
    both = swap(jnp.concatenate([far, near[:, width:]], axis=0), 2)
    return [own, near[:, :width] if cut else near, both]


def swap_x(x, step):
    pairs = []
    for s in range(4 * NZ):
        for d in range(2):
            there = (2 * (s // 2 % 2) + d + step) % 4
            source = s // 4 * 4 + there // 2 * 2 + s % 2
            pairs.append((2 * source + there % 2, 2 * s + d))
    return lax.ppermute(x, SEQ + ("dp",), pairs)


def add(a, b):
    return (a.astype(f32) + b.astype(f32)).astype(bf16)


def per_device(trunk, gains, queries, keys, values, outputs, out_grad, kv_weight):
    seq = lax.axis_index(SEQ)
    info = jnp.stack([seq // 4, seq % 4, lax.axis_index("head"), lax.axis_index("dp")])
    info = info.astype(jnp.int32)
    half = lax.dynamic_slice_in_dim(kv_weight[0], lax.axis_index("dp") * HALF, HALF, 0)
    w_own = lax.all_gather(half, "z", axis=0)
    own, far, send = call(split_kv_body, parts_of(2 * HD), [SMEM, VMEM, VMEM], 0, 1 << 19)(
        info, keys[0, 0], values[0, 0]
    )
    near = swap(send, 1)
    near, query_rows, grad_rows = lax.optimization_barrier((near, queries[0, 0], out_grad[0, 0]))
    both = swap(jnp.concatenate([far, near[:, 2 * HD :]], axis=0), 2)
    kv_own = jnp.concatenate([own, near[:, : 2 * HD], both], axis=0)
    q_cut = call(split_q_body, parts_of(WIDTH), [SMEM, VMEM], 0, 1 << 20)(info, query_rows)
    g_cut = call(split_g_body, parts_of(G_WIDTH), [SMEM, VMEM, VMEM], 0, 1 << 21)(
        info, grad_rows, outputs[0, 0]
    )
    q = rows_of(*q_cut)
    g = rows_of(*g_cut, cut=False)
    blocks = {0: kv_own}
    up = down = kv_own
    carry = ()
    groups = {1: (0,), 2: (1, 7), 3: (2, 6), 4: (3, 5)}
    for k in range(1, 5):
        up = shift(up, 1)
        blocks[k] = up
        if k < 4:
            down = shift(down, -1)
            blocks[NZ - k] = down
        if k == 3:
            carry, w_own = lax.optimization_barrier((carry, w_own))
            w_next, w_last, w_across = [swap_x(w_own, n) for n in (1, 3, 2)]
        carry = stats(groups[k], info, q, blocks, carry)
        if k == 1:
            up, down, q = lax.optimization_barrier((up, down, q))
        elif k == 2:
            up, down, g, carry = lax.optimization_barrier((up, down, g, carry))
        elif k == 3:
            up, carry = lax.optimization_barrier((up, carry))
        if k < 4:
            blocks[k], blocks[NZ - k] = up, down
    row_shift, _, delta = stats((4,), info, q, blocks, carry, g)

    unit = BLOCK * BLOCK * GROUP
    groups = [(4,), (5, 3), (6, 2), (7, 1), (0,)]
    dq_shape = sds((GROUP, HD, BLOCK), f32)
    pair_shape = sds((BLOCK, 2 * HD), bf16)
    dq_parts = [sds((n, WIDTH), bf16) for n in (ROWS, ROWS, 2 * ROWS)]
    acc = pltpu.VMEM((BLOCK, HD), f32)
    dq = ()
    terms = {}
    for n, js in enumerate(groups):
        first, last = n == 0, n == len(groups) - 1
        outs = [pair_shape] * len(js) + (dq_parts if last else [dq_shape])
        operands = [*q, *g, row_shift, delta, *[blocks[j] for j in js], *dq]
        res = call(
            functools.partial(grads_body, js, first, last),
            outs,
            [SMEM] + [VMEM] * len(operands),
            10 * unit * HD * len(js),
            4 << 20,
            scratch=([pltpu.VMEM((GROUP, HD, BLOCK), f32)] if last else []) + [acc, acc],
            exps=unit * len(js),
        )(info, *operands)
        for j, term in zip(js, res):
            terms[j] = term
        dq = tuple(res[len(js) :])
    right = terms[4]
    left = terms[5]
    for k in (4, 3, 2):
        right = add(shift(right, -1), terms[k - 1])
        left = shift(left, 1)
        if k > 2:
            left = add(left, terms[10 - k])
    right = shift(right, -1)
    kv_rows = (terms[0].astype(f32) + right.astype(f32) + left.astype(f32)).astype(bf16)
    kv_rows, w_next, w_last = lax.optimization_barrier((kv_rows, w_next, w_last))
    kv_far = swap(kv_rows[2 * ROWS :], 2)
    kv_far, w_across = lax.optimization_barrier((kv_far, w_across))
    w_parts = [w_own, w_next, w_across, w_last]
    w_parts += [swap(part, 1) for part in w_parts]
    whole = call(
        join_weight_body,
        [sds((NZ, 4, 2 * HALF, 2 * KVH * HD), bf16)],
        [SMEM] + [ANY] * 8,
        0,
        21 << 20,
        scratch=[pltpu.SemaphoreType.DMA((8,))],
        vmem=24,
    )(info, *w_parts)[0]
    kv_near = swap(jnp.concatenate([kv_rows[ROWS : 2 * ROWS], kv_far[ROWS:]], axis=0), 1)

    quarter = sds((ROWS, QUARTER), bf16)
    res = call(
        final_body,
        [quarter] * 4 + [sds((1, D), f32)],
        [SMEM] + [VMEM] * 6,
        2 * ROWS * D * 1024,
        12 << 20,
        scratch=[
            pltpu.VMEM((4, ROWS, QUARTER), f32),
            pltpu.VMEM((ROWS, 2 * KVH * HD), bf16),
        ],
        vmem=24,
    )(info, kv_rows, kv_far, kv_near, trunk[0], gains, whole)
    dq_send, own = lax.optimization_barrier((dq[2], res[0]))
    total = own.astype(f32)
    for d in (1, 2, 3):
        total = total + lax.ppermute(
            res[d], "head", [(y, (y + d) % 4) for y in range(4)]
        ).astype(f32)
    trunk_grad = total.astype(bf16)

    gain = res[4].reshape(D // HD, HD)
    for axes, n in ((("x_hi", "core", "dp"), 8), ("z", NZ)):
        spread = jnp.broadcast_to(gain[None], (n, D // HD, HD))
        gain = jnp.sum(lax.all_to_all(spread, axes, 0, 0, tiled=True), axis=0)
    dq_far = swap(dq_send, 2)
    dq_near = swap(jnp.concatenate([dq[1], dq_far[ROWS:]], axis=0), 1)
    query_grad = call(
        join_q_body, [sds((ROWS, QH * HD), bf16)], [SMEM] + [VMEM] * 3, 0, 1 << 20
    )(info, dq[0], dq_far, dq_near)[0]
    return (query_grad[None, None], trunk_grad[None], gain.reshape(1, D))


def solution(mesh):
    cut = Mesh(
        mesh.devices.reshape(4, NZ, 2, 2, 2), ("head",) + SEQ + ("dp",)
    )
    placed = (
        P("dp", SEQ, None),
        P("head", None),
        P("head", "dp", SEQ, None),
        P("head", "dp", SEQ, None),
        P("head", "dp", SEQ, None),
        P("head", "dp", SEQ, None),
        P("head", "dp", SEQ, None),
        P("head", SEQ, None),
    )
    return jax.shard_map(
        per_device,
        mesh=cut,
        in_specs=placed,
        out_specs=(P("head", "dp", SEQ, None), P("dp", SEQ, "head"), P("head", None)),
        check_vma=False,
    )
```

```python
import functools
import math

import jax
import jax.numpy as jnp
from jax import lax
from jax.experimental import pallas as pl
from jax.experimental.pallas import tpu as pltpu
from jax.sharding import Mesh, PartitionSpec as P

QH = 20
KVH = 4
GROUP = 5
HD = 128
ROWS = 128
EPSILON = 1e-05
SCALE = 1.0 / math.sqrt(HD)
EXP_SCALE = SCALE * math.log2(math.e)
NZ = 8
BLOCK = 4 * ROWS
D = 5120
QUARTER = D // 4
HALF = 80
TILE = 256
SEQ = ("z", "x_hi", "core")
WIDTH = GROUP * HD
G_WIDTH = WIDTH + HD
bf16 = jnp.bfloat16
f32 = jnp.float32

SMEM = pl.BlockSpec(memory_space=pltpu.SMEM)
VMEM = pl.BlockSpec(memory_space=pltpu.VMEM)
ANY = pl.BlockSpec(memory_space=pl.ANY)
NT = (((1,), (1,)), ((), ()))
TN = (((0,), (0,)), ((), ()))


def call(body, out_shape, in_specs, flops, nbytes, scratch=(), exps=0, vmem=16):
    return pl.pallas_call(
        body,
        out_shape=out_shape,
        in_specs=in_specs,
        out_specs=[VMEM] * len(out_shape),
        scratch_shapes=list(scratch),
        compiler_params=pltpu.CompilerParams(vmem_limit_bytes=vmem * 1024 * 1024),
        cost_estimate=pl.CostEstimate(flops=flops, bytes_accessed=nbytes, transcendentals=exps),
    )


def sds(shape, dtype):
    return jax.ShapeDtypeStruct(shape, dtype)


def split_kv_body(info, k, v, own, far, send):
    i = info[1]
    for p, (out, start) in enumerate(((own, 0), (send, 0), (far, 0), (send, 2 * HD))):
        cols = pl.ds(pl.multiple_of((i ^ p) * HD, HD), HD)
        out[:, start : start + HD] = k[:, cols]
        out[:, start + HD : start + 2 * HD] = v[:, cols]


def split_q_body(info, q, own, far, send):
    i = info[1]
    for p, (out, start) in enumerate(((own, 0), (send, 0), (far, 0), (send, WIDTH))):
        cols = pl.ds(pl.multiple_of((i ^ p) * WIDTH, HD), WIDTH)
        out[:, start : start + WIDTH] = q[:, cols]


def split_g_body(info, g, o, own, far, send):
    i = info[1]
    lane = lax.broadcasted_iota(jnp.int32, (ROWS, HD), 1)
    for p, (out, start) in enumerate(((own, 0), (send, 0), (far, 0), (send, G_WIDTH))):
        first = pl.multiple_of((i ^ p) * WIDTH, HD)
        out[:, start : start + WIDTH] = g[:, pl.ds(first, WIDTH)]
        coded = jnp.zeros((ROWS, HD), f32)
        for h in range(GROUP):
            head = pl.ds(pl.multiple_of(first + h * HD, HD), HD)
            product = g[:, head].astype(f32) * o[:, head].astype(f32)
            total = jnp.sum(product, axis=1, keepdims=True)
            for part in range(3):
                rounded = total.astype(bf16).astype(f32)
                coded = jnp.where(lane == 8 * part + h, rounded, coded)
                total = total - rounded
        out[:, start + WIDTH : start + G_WIDTH] = coded.astype(bf16)


def head_rows(pieces, h):
    cols = pl.ds(pl.multiple_of(h * HD, HD), HD)
    return jnp.concatenate([piece[:, cols] for piece in pieces], axis=0)


def causal_mask(i, u, rows, t):
    row = lax.broadcasted_iota(jnp.int32, (rows, TILE), 0) + u
    col = lax.broadcasted_iota(jnp.int32, (rows, TILE), 1) + t
    key_pos = row ^ (i * ROWS)
    query_pos = col ^ (i * ROWS)
    return key_pos <= query_pos


def stats_body(js, first, last, has_g, info, *refs):
    z, i = info[0], info[1]
    q = refs[:3]
    if has_g:
        g = refs[3:6]
        refs = refs[3:]
    keys = refs[3 : 3 + len(js)]
    rest = refs[3 + len(js) :]
    if has_g:
        delta_ref = rest[-1]
        rest = rest[:-1]
    if first:
        m_ref, l_ref = rest
        m_ref[...] = jnp.full(m_ref.shape, -1e30, f32)
        l_ref[...] = jnp.zeros(l_ref.shape, f32)
    else:
        m_in, l_in, m_ref, l_ref = rest
        m_ref[...] = m_in[...]
        l_ref[...] = l_in[...]
    for j, key in zip(js, keys):

        @pl.when(j <= z)
        def _(j=j, key=key):
            for h in range(GROUP):
                for t in range(0, BLOCK, TILE):
                    heads = head_rows(q, h)[t : t + TILE]
                    cols = slice(t, t + TILE)
                    m, total = m_ref[h : h + 1, cols], l_ref[h : h + 1, cols]
                    for u in range(0, BLOCK, ROWS):
                        scores = lax.dot_general(
                            key[u : u + ROWS, :HD], heads, NT, preferred_element_type=f32
                        )
                        if j == 0:
                            scores = jnp.where(causal_mask(i, u, ROWS, t), scores, -1e30)
                        m_new = jnp.maximum(m, jnp.max(scores, axis=0, keepdims=True))
                        shift = m_new * EXP_SCALE
                        total = total * jnp.exp2(m * EXP_SCALE - shift) + jnp.sum(
                            jnp.exp2(scores * EXP_SCALE - shift), axis=0, keepdims=True
                        )
                        m = m_new
                    m_ref[h : h + 1, cols] = m
                    l_ref[h : h + 1, cols] = total

    if last:
        l_ref[...] = jnp.where(l_ref[...] > 0.0, l_ref[...], 1.0)
        m_ref[...] = m_ref[...] * EXP_SCALE + jnp.log2(l_ref[...])
    if has_g:
        for p, (piece, start) in enumerate(((g[0], 0), (g[1], 0), (g[2], 0), (g[2], ROWS))):
            coded = piece[start : start + ROWS, WIDTH:G_WIDTH].astype(f32).T
            delta_ref[:, p * ROWS : (p + 1) * ROWS] = coded[:8] + coded[8:16] + coded[16:24]


def grads_body(js, first, last, info, *refs):
    z, i = info[0], info[1]
    n = len(js)
    q, g = refs[:3], refs[3:6]
    shift_ref, delta_ref = refs[6:8]
    blocks = refs[8 : 8 + n]
    rest = refs[8 + n :]
    if not first:
        dq_in, rest = rest[0], rest[1:]
    outs = rest[:n]
    rest = rest[n:]
    if last:
        dq_outs, rest = rest[:3], rest[3:]
        dq, dk, dv = rest
        dq[...] = dq_in[...]
    else:
        dq, dk, dv = rest
        if first:
            dq[...] = jnp.zeros(dq.shape, f32)
        else:
            dq[...] = dq_in[...]
    for j, block, out in zip(js, blocks, outs):

        @pl.when(j <= z)
        def _(j=j, block=block, out=out):
            key, value = block[:, :HD], block[:, HD:]
            dk[...] = jnp.zeros(dk.shape, f32)
            dv[...] = jnp.zeros(dv.shape, f32)
            for h in range(GROUP):
                qh = head_rows(q, h)
                gh = head_rows(g, h)
                for t in range(0, BLOCK, TILE):
                    cols = slice(t, t + TILE)
                    row = pl.ds(h, 1)
                    scores = lax.dot_general(key, qh[cols], NT, preferred_element_type=f32)
                    probs = jnp.exp2(scores * EXP_SCALE - shift_ref[row, cols])
                    if j == 0:
                        probs = jnp.where(causal_mask(i, 0, BLOCK, t), probs, 0.0)
                    dprobs = lax.dot_general(value, gh[cols], NT, preferred_element_type=f32)
                    dscores = (probs * (dprobs - delta_ref[row, cols])).astype(bf16)
                    dv_part = jnp.dot(probs.astype(bf16), gh[cols], preferred_element_type=f32)
                    dk_part = jnp.dot(dscores, qh[cols], preferred_element_type=f32)
                    dv[...] += dv_part
                    dk[...] += dk_part
                    dq[h, :, cols] += lax.dot_general(key, dscores, TN, preferred_element_type=f32)
            out[:, :HD] = (dk[...] * SCALE).astype(bf16)
            out[:, HD:] = dv[...].astype(bf16)

        @pl.when(j > z)
        def _(out=out):
            out[...] = jnp.zeros(out.shape, bf16)

    if last:
        for out, start in zip(dq_outs, (0, ROWS, 2 * ROWS)):
            for h in range(GROUP):
                rows = dq[h, :, start : start + out.shape[0]].T
                out[:, h * HD : (h + 1) * HD] = (rows * SCALE).astype(bf16)


def join_q_body(info, own, far, near, out):
    i = info[1]
    for p, (piece, start) in enumerate(((own, 0), (near, 0), (far, 0), (near, ROWS))):
        cols = pl.ds(pl.multiple_of((i ^ p) * WIDTH, HD), WIDTH)
        out[:, cols] = piece[start : start + ROWS, :]


def join_weight_body(info, *refs):
    i, dp = info[1], info[3]
    whole, sems = refs[8:]
    copies = []
    for n in range(8):
        x = lax.rem(i // 2 * 2 + dp + n % 4, 4)
        block = x // 2 * 2 + (i % 2 if n < 4 else 1 - i % 2)
        place = pl.ds(pl.multiple_of(x % 2 * HALF, 16), HALF)
        copies.append(
            pltpu.make_async_copy(refs[n], whole.at[:, block, place, :], sems.at[n])
        )
        copies[n].start()
    for copy in copies:
        copy.wait()


def final_body(info, own, far, near, trunk, gains, whole, *refs):
    i, y = info[1], info[2]
    outs, (gain_out, proj, left) = refs[:4], refs[4:]
    for p, (piece, start) in enumerate(((own, 0), (near, 0), (far, 0), (near, ROWS))):
        head = i ^ p
        rows = slice(start, start + ROWS)
        left[:, pl.ds(pl.multiple_of(head * HD, HD), HD)] = piece[rows, :HD]
        left[:, pl.ds(pl.multiple_of(KVH * HD + head * HD, HD), HD)] = piece[rows, HD:]
    squares = jnp.zeros((ROWS, 1), f32)
    for d in range(4):
        hidden = trunk[:, d * QUARTER : (d + 1) * QUARTER].astype(f32)
        squares = squares + jnp.sum(hidden * hidden, axis=1, keepdims=True)
    inverse = lax.rsqrt(squares * (1.0 / D) + EPSILON)
    row_stat = jnp.zeros((ROWS, 1), f32)
    for d in range(4):
        cols = pl.ds(pl.multiple_of(lax.rem(y + d, 4) * QUARTER, QUARTER), QUARTER)
        weight = whole[pl.ds(2 * lax.rem(y + d, 4), 2)].reshape(QUARTER, 2 * KVH * HD)
        part = lax.dot_general(left[...], weight, NT, preferred_element_type=f32)
        normed = trunk[:, cols].astype(f32) * inverse
        product = part * normed
        gain_out[:, cols] = jnp.sum(product, axis=0, keepdims=True)
        row_stat = row_stat + jnp.sum(product * gains[:, cols], axis=1, keepdims=True)
        proj[d] = part
    row_stat = row_stat * (1.0 / D)
    for d in range(4):
        cols = pl.ds(pl.multiple_of(lax.rem(y + d, 4) * QUARTER, QUARTER), QUARTER)
        normed = trunk[:, cols].astype(f32) * inverse
        outs[d][...] = ((gains[:, cols] * proj[d] - normed * row_stat) * inverse).astype(bf16)


def seq_permute(x, pairs):
    return lax.ppermute(x, SEQ, pairs)


def swap(x, p):
    return seq_permute(x, [(s, s ^ p) for s in range(4 * NZ)])


def shift(x, step):
    return seq_permute(x, [(s, (s + 4 * step) % (4 * NZ)) for s in range(4 * NZ)])


def stats(js, info, q, blocks, carry, g=(), last=False):
    unit = BLOCK * BLOCK * GROUP * len(js)
    stat = sds((8, BLOCK), f32)
    operands = [*q, *g, *[blocks[j] for j in js], *carry]
    return call(
        functools.partial(stats_body, js, not carry, last, bool(g)),
        [stat] * (3 if g else 2),
        [SMEM] + [VMEM] * len(operands),
        2 * unit * HD,
        1 << 20,
        exps=unit,
    )(info, *operands)


def parts_of(width):
    return [sds((ROWS, width), bf16), sds((ROWS, width), bf16), sds((ROWS, 2 * width), bf16)]


def rows_of(own, far, send, cut=True):
    width = own.shape[1]
    near = swap(send, 1)
    both = swap(jnp.concatenate([far, near[:, width:]], axis=0), 2)
    return [own, near[:, :width] if cut else near, both]


def swap_x(x, step):
    pairs = []
    for s in range(4 * NZ):
        for d in range(2):
            there = (2 * (s // 2 % 2) + d + step) % 4
            source = s // 4 * 4 + there // 2 * 2 + s % 2
            pairs.append((2 * source + there % 2, 2 * s + d))
    return lax.ppermute(x, SEQ + ("dp",), pairs)


def add(a, b):
    return (a.astype(f32) + b.astype(f32)).astype(bf16)


def per_device(trunk, gains, queries, keys, values, outputs, out_grad, kv_weight):
    seq = lax.axis_index(SEQ)
    info = jnp.stack([seq // 4, seq % 4, lax.axis_index("head"), lax.axis_index("dp")])
    info = info.astype(jnp.int32)
    half = lax.dynamic_slice_in_dim(kv_weight[0], lax.axis_index("dp") * HALF, HALF, 0)
    w_own = lax.all_gather(half, "z", axis=0)
    own, far, send = call(split_kv_body, parts_of(2 * HD), [SMEM, VMEM, VMEM], 0, 1 << 19)(
        info, keys[0, 0], values[0, 0]
    )
    near = swap(send, 1)
    near, query_rows, grad_rows = lax.optimization_barrier((near, queries[0, 0], out_grad[0, 0]))
    both = swap(jnp.concatenate([far, near[:, 2 * HD :]], axis=0), 2)
    kv_own = jnp.concatenate([own, near[:, : 2 * HD], both], axis=0)
    q_cut = call(split_q_body, parts_of(WIDTH), [SMEM, VMEM], 0, 1 << 20)(info, query_rows)
    g_cut = call(split_g_body, parts_of(G_WIDTH), [SMEM, VMEM, VMEM], 0, 1 << 21)(
        info, grad_rows, outputs[0, 0]
    )
    q = rows_of(*q_cut)
    g = rows_of(*g_cut, cut=False)
    blocks = {0: kv_own}
    up = down = kv_own
    carry = ()
    groups = {1: (0,), 2: (1, 7), 3: (2, 6), 4: (3, 5)}
    for k in range(1, 5):
        up = shift(up, 1)
        blocks[k] = up
        if k < 4:
            down = shift(down, -1)
            blocks[NZ - k] = down
        if k == 3:
            carry, w_own = lax.optimization_barrier((carry, w_own))
            w_next, w_last = swap_x(w_own, 1), swap_x(w_own, 3)
        carry = stats(groups[k], info, q, blocks, carry, g if k == 2 else ())
        if k == 2:
            carry, delta = carry[:2], carry[2]
        if k == 1:
            up, down, q = lax.optimization_barrier((up, down, q))
        elif k == 2:
            up, down, g, carry = lax.optimization_barrier((up, down, g, carry))
        elif k == 3:
            up, carry = lax.optimization_barrier((up, carry))
        if k < 4:
            blocks[k], blocks[NZ - k] = up, down
    row_shift, _ = stats((4,), info, q, blocks, carry, last=True)

    unit = BLOCK * BLOCK * GROUP
    groups = [(4,), (5, 3), (6, 2), (7, 1), (0,)]
    dq_shape = sds((GROUP, HD, BLOCK), f32)
    pair_shape = sds((BLOCK, 2 * HD), bf16)
    dq_parts = [sds((n, WIDTH), bf16) for n in (ROWS, ROWS, 2 * ROWS)]
    acc = pltpu.VMEM((BLOCK, HD), f32)
    dq = ()
    terms = {}
    for n, js in enumerate(groups):
        first, last = n == 0, n == len(groups) - 1
        if n == 2:
            w_sent, dq = lax.optimization_barrier((w_own, dq))
            w_across = swap_x(w_sent, 2)
        outs = [pair_shape] * len(js) + (dq_parts if last else [dq_shape])
        operands = [*q, *g, row_shift, delta, *[blocks[j] for j in js], *dq]
        res = call(
            functools.partial(grads_body, js, first, last),
            outs,
            [SMEM] + [VMEM] * len(operands),
            10 * unit * HD * len(js),
            4 << 20,
            scratch=([pltpu.VMEM((GROUP, HD, BLOCK), f32)] if last else []) + [acc, acc],
            exps=unit * len(js),
        )(info, *operands)
        for j, term in zip(js, res):
            terms[j] = term
        dq = tuple(res[len(js) :])
    right = terms[4]
    left = terms[5]
    for k in (4, 3, 2):
        right = add(shift(right, -1), terms[k - 1])
        left = shift(left, 1)
        if k > 2:
            left = add(left, terms[10 - k])
    right = shift(right, -1)
    kv_rows = (terms[0].astype(f32) + right.astype(f32) + left.astype(f32)).astype(bf16)
    kv_rows, w_next, w_last = lax.optimization_barrier((kv_rows, w_next, w_last))
    kv_far = swap(kv_rows[2 * ROWS :], 2)
    kv_far, w_across = lax.optimization_barrier((kv_far, w_across))
    w_parts = [w_own, w_next, w_across, w_last]
    w_parts += [swap(part, 1) for part in w_parts]
    whole = call(
        join_weight_body,
        [sds((NZ, 4, 2 * HALF, 2 * KVH * HD), bf16)],
        [SMEM] + [ANY] * 8,
        0,
        21 << 20,
        scratch=[pltpu.SemaphoreType.DMA((8,))],
        vmem=24,
    )(info, *w_parts)[0]
    kv_near = swap(jnp.concatenate([kv_rows[ROWS : 2 * ROWS], kv_far[ROWS:]], axis=0), 1)

    quarter = sds((ROWS, QUARTER), bf16)
    res = call(
        final_body,
        [quarter] * 4 + [sds((1, D), f32)],
        [SMEM] + [VMEM] * 6,
        2 * ROWS * D * 1024,
        12 << 20,
        scratch=[
            pltpu.VMEM((4, ROWS, QUARTER), f32),
            pltpu.VMEM((ROWS, 2 * KVH * HD), bf16),
        ],
        vmem=24,
    )(info, kv_rows, kv_far, kv_near, trunk[0], gains, whole)
    dq_send, own = lax.optimization_barrier((dq[2], res[0]))
    total = own.astype(f32)
    for d in (1, 2, 3):
        total = total + lax.ppermute(
            res[d], "head", [(y, (y + d) % 4) for y in range(4)]
        ).astype(f32)
    trunk_grad = total.astype(bf16)

    gain = res[4].reshape(D // HD, HD)
    gain = gain + swap(gain, 1)
    beside = swap_x(gain, 1) + swap_x(gain, 3)
    gain = (gain + swap_x(gain, 2)) + beside
    spread = jnp.broadcast_to(gain[None], (NZ, D // HD, HD))
    gains_of_z = lax.all_to_all(spread, "z", 0, 0, tiled=True)
    dq_far = swap(dq_send, 2)
    dq_near = swap(jnp.concatenate([dq[1], dq_far[ROWS:]], axis=0), 1)
    query_grad = call(
        join_q_body, [sds((ROWS, QH * HD), bf16)], [SMEM] + [VMEM] * 3, 0, 1 << 20
    )(info, dq[0], dq_far, dq_near)[0]
    gains_of_z, query_grad = lax.optimization_barrier((gains_of_z, query_grad))
    gain = jnp.sum(gains_of_z, axis=0)
    return (query_grad[None, None], trunk_grad[None], gain.reshape(1, D))


def solution(mesh):
    cut = Mesh(
        mesh.devices.reshape(4, NZ, 2, 2, 2), ("head",) + SEQ + ("dp",)
    )
    placed = (
        P("dp", SEQ, None),
        P("head", None),
        P("head", "dp", SEQ, None),
        P("head", "dp", SEQ, None),
        P("head", "dp", SEQ, None),
        P("head", "dp", SEQ, None),
        P("head", "dp", SEQ, None),
        P("head", SEQ, None),
    )
    return jax.shard_map(
        per_device,
        mesh=cut,
        in_specs=placed,
        out_specs=(P("head", "dp", SEQ, None), P("dp", SEQ, "head"), P("head", None)),
        check_vma=False,
    )
```

```python
import functools
import math

import jax
import jax.numpy as jnp
from jax import lax
from jax.experimental import pallas as pl
from jax.experimental.pallas import tpu as pltpu
from jax.sharding import Mesh, PartitionSpec as P

QH = 20
KVH = 4
GROUP = 5
HD = 128
ROWS = 128
EPSILON = 1e-05
SCALE = 1.0 / math.sqrt(HD)
EXP_SCALE = SCALE * math.log2(math.e)
NZ = 8
BLOCK = 4 * ROWS
D = 5120
QUARTER = D // 4
HALF = 80
TILE = 256
SEQ = ("z", "x_hi", "core")
WIDTH = GROUP * HD
G_WIDTH = WIDTH + HD
bf16 = jnp.bfloat16
f32 = jnp.float32

SMEM = pl.BlockSpec(memory_space=pltpu.SMEM)
VMEM = pl.BlockSpec(memory_space=pltpu.VMEM)
ANY = pl.BlockSpec(memory_space=pl.ANY)
NT = (((1,), (1,)), ((), ()))
TN = (((0,), (0,)), ((), ()))


def call(body, out_shape, in_specs, flops, nbytes, scratch=(), exps=0, vmem=16):
    return pl.pallas_call(
        body,
        out_shape=out_shape,
        in_specs=in_specs,
        out_specs=[VMEM] * len(out_shape),
        scratch_shapes=list(scratch),
        compiler_params=pltpu.CompilerParams(vmem_limit_bytes=vmem * 1024 * 1024),
        cost_estimate=pl.CostEstimate(flops=flops, bytes_accessed=nbytes, transcendentals=exps),
    )


def sds(shape, dtype):
    return jax.ShapeDtypeStruct(shape, dtype)


def split_kv_body(info, k, v, own, far, send):
    i = info[1]
    for p, (out, start) in enumerate(((own, 0), (send, 0), (far, 0), (send, 2 * HD))):
        cols = pl.ds(pl.multiple_of((i ^ p) * HD, HD), HD)
        out[:, start : start + HD] = k[:, cols]
        out[:, start + HD : start + 2 * HD] = v[:, cols]


def split_q_body(info, q, own, far, send):
    i = info[1]
    for p, (out, start) in enumerate(((own, 0), (send, 0), (far, 0), (send, WIDTH))):
        cols = pl.ds(pl.multiple_of((i ^ p) * WIDTH, HD), WIDTH)
        out[:, start : start + WIDTH] = q[:, cols]


def split_g_body(info, g, o, own, far, send):
    i = info[1]
    lane = lax.broadcasted_iota(jnp.int32, (ROWS, HD), 1)
    for p, (out, start) in enumerate(((own, 0), (send, 0), (far, 0), (send, G_WIDTH))):
        first = pl.multiple_of((i ^ p) * WIDTH, HD)
        out[:, start : start + WIDTH] = g[:, pl.ds(first, WIDTH)]
        coded = jnp.zeros((ROWS, HD), f32)
        for h in range(GROUP):
            head = pl.ds(pl.multiple_of(first + h * HD, HD), HD)
            product = g[:, head].astype(f32) * o[:, head].astype(f32)
            total = jnp.sum(product, axis=1, keepdims=True)
            for part in range(3):
                rounded = total.astype(bf16).astype(f32)
                coded = jnp.where(lane == 8 * part + h, rounded, coded)
                total = total - rounded
        out[:, start + WIDTH : start + G_WIDTH] = coded.astype(bf16)


def head_rows(pieces, h):
    cols = pl.ds(pl.multiple_of(h * HD, HD), HD)
    return jnp.concatenate([piece[:, cols] for piece in pieces], axis=0)


def causal_mask(i, u, rows, t):
    row = lax.broadcasted_iota(jnp.int32, (rows, TILE), 0) + u
    col = lax.broadcasted_iota(jnp.int32, (rows, TILE), 1) + t
    key_pos = row ^ (i * ROWS)
    query_pos = col ^ (i * ROWS)
    return key_pos <= query_pos


def stats_body(js, first, last, has_g, info, *refs):
    z, i = info[0], info[1]
    q = refs[:3]
    if has_g:
        g = refs[3:6]
        refs = refs[3:]
    keys = refs[3 : 3 + len(js)]
    rest = refs[3 + len(js) :]
    if has_g:
        delta_ref = rest[-1]
        rest = rest[:-1]
    if first:
        m_ref, l_ref = rest
        m_ref[...] = jnp.full(m_ref.shape, -1e30, f32)
        l_ref[...] = jnp.zeros(l_ref.shape, f32)
    else:
        m_in, l_in, m_ref, l_ref = rest
        m_ref[...] = m_in[...]
        l_ref[...] = l_in[...]
    for j, key in zip(js, keys):

        @pl.when(j <= z)
        def _(j=j, key=key):
            for h in range(GROUP):
                for t in range(0, BLOCK, TILE):
                    heads = head_rows(q, h)[t : t + TILE]
                    cols = slice(t, t + TILE)
                    m, total = m_ref[h : h + 1, cols], l_ref[h : h + 1, cols]
                    for u in range(0, BLOCK, ROWS):
                        scores = lax.dot_general(
                            key[u : u + ROWS, :HD], heads, NT, preferred_element_type=f32
                        )
                        if j == 0:
                            scores = jnp.where(causal_mask(i, u, ROWS, t), scores, -1e30)
                        m_new = jnp.maximum(m, jnp.max(scores, axis=0, keepdims=True))
                        shift = m_new * EXP_SCALE
                        total = total * jnp.exp2(m * EXP_SCALE - shift) + jnp.sum(
                            jnp.exp2(scores * EXP_SCALE - shift), axis=0, keepdims=True
                        )
                        m = m_new
                    m_ref[h : h + 1, cols] = m
                    l_ref[h : h + 1, cols] = total

    if last:
        l_ref[...] = jnp.where(l_ref[...] > 0.0, l_ref[...], 1.0)
        m_ref[...] = m_ref[...] * EXP_SCALE + jnp.log2(l_ref[...])
    if has_g:
        for p, (piece, start) in enumerate(((g[0], 0), (g[1], 0), (g[2], 0), (g[2], ROWS))):
            coded = piece[start : start + ROWS, WIDTH:G_WIDTH].astype(f32).T
            delta_ref[:, p * ROWS : (p + 1) * ROWS] = coded[:8] + coded[8:16] + coded[16:24]


def grads_body(js, first, last, info, *refs):
    z, i = info[0], info[1]
    n = len(js)
    q, g = refs[:3], refs[3:6]
    shift_ref, delta_ref = refs[6:8]
    blocks = refs[8 : 8 + n]
    rest = refs[8 + n :]
    if not first:
        dq_in, rest = rest[0], rest[1:]
    outs = rest[:n]
    rest = rest[n:]
    if last:
        dq_outs, rest = rest[:3], rest[3:]
        dq, dk, dv = rest
        dq[...] = dq_in[...]
    else:
        dq, dk, dv = rest
        if first:
            dq[...] = jnp.zeros(dq.shape, f32)
        else:
            dq[...] = dq_in[...]
    for j, block, out in zip(js, blocks, outs):

        @pl.when(j <= z)
        def _(j=j, block=block, out=out):
            key, value = block[:, :HD], block[:, HD:]
            dk[...] = jnp.zeros(dk.shape, f32)
            dv[...] = jnp.zeros(dv.shape, f32)
            for h in range(GROUP):
                qh = head_rows(q, h)
                gh = head_rows(g, h)
                for t in range(0, BLOCK, TILE):
                    cols = slice(t, t + TILE)
                    row = pl.ds(h, 1)
                    scores = lax.dot_general(key, qh[cols], NT, preferred_element_type=f32)
                    probs = jnp.exp2(scores * EXP_SCALE - shift_ref[row, cols])
                    if j == 0:
                        probs = jnp.where(causal_mask(i, 0, BLOCK, t), probs, 0.0)
                    dprobs = lax.dot_general(value, gh[cols], NT, preferred_element_type=f32)
                    dscores = (probs * (dprobs - delta_ref[row, cols])).astype(bf16)
                    dv_part = jnp.dot(probs.astype(bf16), gh[cols], preferred_element_type=f32)
                    dk_part = jnp.dot(dscores, qh[cols], preferred_element_type=f32)
                    dv[...] += dv_part
                    dk[...] += dk_part
                    dq[h, :, cols] += lax.dot_general(key, dscores, TN, preferred_element_type=f32)
            out[:, :HD] = (dk[...] * SCALE).astype(bf16)
            out[:, HD:] = dv[...].astype(bf16)

        @pl.when(j > z)
        def _(out=out):
            out[...] = jnp.zeros(out.shape, bf16)

    if last:
        for out, start in zip(dq_outs, (0, ROWS, 2 * ROWS)):
            for h in range(GROUP):
                rows = dq[h, :, start : start + out.shape[0]].T
                out[:, h * HD : (h + 1) * HD] = (rows * SCALE).astype(bf16)


def join_q_body(info, own, far, near, out):
    i = info[1]
    for p, (piece, start) in enumerate(((own, 0), (near, 0), (far, 0), (near, ROWS))):
        cols = pl.ds(pl.multiple_of((i ^ p) * WIDTH, HD), WIDTH)
        out[:, cols] = piece[start : start + ROWS, :]


def join_weight_body(info, *refs):
    i, dp = info[1], info[3]
    whole, sems = refs[8:]
    copies = []
    for n in range(8):
        x = lax.rem(i // 2 * 2 + dp + n % 4, 4)
        block = x // 2 * 2 + (i % 2 if n < 4 else 1 - i % 2)
        place = pl.ds(pl.multiple_of(x % 2 * HALF, 16), HALF)
        copies.append(
            pltpu.make_async_copy(refs[n], whole.at[:, block, place, :], sems.at[n])
        )
        copies[n].start()
    for copy in copies:
        copy.wait()


def final_body(info, own, far, near, trunk, gains, whole, *refs):
    i, y = info[1], info[2]
    outs, (gain_out, proj, left) = refs[:4], refs[4:]
    for p, (piece, start) in enumerate(((own, 0), (near, 0), (far, 0), (near, ROWS))):
        head = i ^ p
        rows = slice(start, start + ROWS)
        left[:, pl.ds(pl.multiple_of(head * HD, HD), HD)] = piece[rows, :HD]
        left[:, pl.ds(pl.multiple_of(KVH * HD + head * HD, HD), HD)] = piece[rows, HD:]
    squares = jnp.zeros((ROWS, 1), f32)
    for d in range(4):
        hidden = trunk[:, d * QUARTER : (d + 1) * QUARTER].astype(f32)
        squares = squares + jnp.sum(hidden * hidden, axis=1, keepdims=True)
    inverse = lax.rsqrt(squares * (1.0 / D) + EPSILON)
    row_stat = jnp.zeros((ROWS, 1), f32)
    for d in range(4):
        cols = pl.ds(pl.multiple_of(lax.rem(y + d, 4) * QUARTER, QUARTER), QUARTER)
        weight = whole[pl.ds(2 * lax.rem(y + d, 4), 2)].reshape(QUARTER, 2 * KVH * HD)
        part = lax.dot_general(left[...], weight, NT, preferred_element_type=f32)
        normed = trunk[:, cols].astype(f32) * inverse
        product = part * normed
        gain_out[:, cols] = jnp.sum(product, axis=0, keepdims=True)
        row_stat = row_stat + jnp.sum(product * gains[:, cols], axis=1, keepdims=True)
        proj[d] = part
    row_stat = row_stat * (1.0 / D)
    for d in range(4):
        cols = pl.ds(pl.multiple_of(lax.rem(y + d, 4) * QUARTER, QUARTER), QUARTER)
        normed = trunk[:, cols].astype(f32) * inverse
        outs[d][...] = ((gains[:, cols] * proj[d] - normed * row_stat) * inverse).astype(bf16)


def seq_permute(x, pairs):
    return lax.ppermute(x, SEQ, pairs)


def swap(x, p):
    return seq_permute(x, [(s, s ^ p) for s in range(4 * NZ)])


def shift(x, step, sources=range(NZ)):
    seqs = [4 * (z % NZ) + i for z in sources for i in range(4)]
    return seq_permute(x, [(s, (s + 4 * step) % (4 * NZ)) for s in seqs])


def stats(js, info, q, blocks, carry, g=(), last=False):
    unit = BLOCK * BLOCK * GROUP * len(js)
    stat = sds((8, BLOCK), f32)
    operands = [*q, *g, *[blocks[j] for j in js], *carry]
    return call(
        functools.partial(stats_body, js, not carry, last, bool(g)),
        [stat] * (3 if g else 2),
        [SMEM] + [VMEM] * len(operands),
        2 * unit * HD,
        1 << 20,
        exps=unit,
    )(info, *operands)


def parts_of(width):
    return [sds((ROWS, width), bf16), sds((ROWS, width), bf16), sds((ROWS, 2 * width), bf16)]


def rows_of(own, far, send, cut=True):
    width = own.shape[1]
    near = swap(send, 1)
    both = swap(jnp.concatenate([far, near[:, width:]], axis=0), 2)
    return [own, near[:, :width] if cut else near, both]


def swap_x(x, step):
    pairs = []
    for s in range(4 * NZ):
        for d in range(2):
            there = (2 * (s // 2 % 2) + d + step) % 4
            source = s // 4 * 4 + there // 2 * 2 + s % 2
            pairs.append((2 * source + there % 2, 2 * s + d))
    return lax.ppermute(x, SEQ + ("dp",), pairs)


def add(a, b):
    return (a.astype(f32) + b.astype(f32)).astype(bf16)


def per_device(trunk, gains, queries, keys, values, outputs, out_grad, kv_weight):
    seq = lax.axis_index(SEQ)
    info = jnp.stack([seq // 4, seq % 4, lax.axis_index("head"), lax.axis_index("dp")])
    info = info.astype(jnp.int32)
    half = lax.dynamic_slice_in_dim(kv_weight[0], lax.axis_index("dp") * HALF, HALF, 0)
    w_own = lax.all_gather(half, "z", axis=0)
    own, far, send = call(split_kv_body, parts_of(2 * HD), [SMEM, VMEM, VMEM], 0, 1 << 19)(
        info, keys[0, 0], values[0, 0]
    )
    near = swap(send, 1)
    near, query_rows, grad_rows = lax.optimization_barrier((near, queries[0, 0], out_grad[0, 0]))
    both = swap(jnp.concatenate([far, near[:, 2 * HD :]], axis=0), 2)
    kv_own = jnp.concatenate([own, near[:, : 2 * HD], both], axis=0)
    q_cut = call(split_q_body, parts_of(WIDTH), [SMEM, VMEM], 0, 1 << 20)(info, query_rows)
    g_cut = call(split_g_body, parts_of(G_WIDTH), [SMEM, VMEM, VMEM], 0, 1 << 21)(
        info, grad_rows, outputs[0, 0]
    )
    q = rows_of(*q_cut)
    g = rows_of(*g_cut, cut=False)
    blocks = {0: kv_own}
    up = down = kv_own
    carry = ()
    groups = {1: (0,), 2: (1, 7), 3: (2, 6), 4: (3, 5)}
    for k in range(1, 5):
        up = shift(up, 1)
        blocks[k] = up
        if k < 4:
            down = shift(down, -1, [b - k + 1 for b in range(3)] if k < 3 else range(NZ))
            blocks[NZ - k] = down
        if k == 3:
            carry, w_own = lax.optimization_barrier((carry, w_own))
            w_next, w_last = swap_x(w_own, 1), swap_x(w_own, 3)
        carry = stats(groups[k], info, q, blocks, carry, g if k == 2 else ())
        if k == 2:
            carry, delta = carry[:2], carry[2]
        if k == 1:
            up, down, q = lax.optimization_barrier((up, down, q))
        elif k == 2:
            up, down, g, carry = lax.optimization_barrier((up, down, g, carry))
        elif k == 3:
            up, carry = lax.optimization_barrier((up, carry))
        if k < 4:
            blocks[k], blocks[NZ - k] = up, down
    row_shift, _ = stats((4,), info, q, blocks, carry, last=True)

    unit = BLOCK * BLOCK * GROUP
    groups = [(4,), (5, 3), (6, 2), (7, 1), (0,)]
    dq_shape = sds((GROUP, HD, BLOCK), f32)
    pair_shape = sds((BLOCK, 2 * HD), bf16)
    dq_parts = [sds((n, WIDTH), bf16) for n in (ROWS, ROWS, 2 * ROWS)]
    acc = pltpu.VMEM((BLOCK, HD), f32)
    dq = ()
    terms = {}
    for n, js in enumerate(groups):
        first, last = n == 0, n == len(groups) - 1
        if n == 2:
            w_sent, dq = lax.optimization_barrier((w_own, dq))
            w_across = swap_x(w_sent, 2)
        outs = [pair_shape] * len(js) + (dq_parts if last else [dq_shape])
        operands = [*q, *g, row_shift, delta, *[blocks[j] for j in js], *dq]
        res = call(
            functools.partial(grads_body, js, first, last),
            outs,
            [SMEM] + [VMEM] * len(operands),
            10 * unit * HD * len(js),
            4 << 20,
            scratch=([pltpu.VMEM((GROUP, HD, BLOCK), f32)] if last else []) + [acc, acc],
            exps=unit * len(js),
        )(info, *operands)
        for j, term in zip(js, res):
            terms[j] = term
        dq = tuple(res[len(js) :])
    right = terms[4]
    left = terms[5]
    for k in (4, 3, 2):
        right = add(shift(right, -1), terms[k - 1])
        left = shift(left, 1)
        if k > 2:
            left = add(left, terms[10 - k])
    right = shift(right, -1)
    kv_rows = (terms[0].astype(f32) + right.astype(f32) + left.astype(f32)).astype(bf16)
    kv_rows, w_next, w_last = lax.optimization_barrier((kv_rows, w_next, w_last))
    kv_far = swap(kv_rows[2 * ROWS :], 2)
    kv_far, w_across = lax.optimization_barrier((kv_far, w_across))
    w_parts = [w_own, w_next, w_across, w_last]
    w_parts += [swap(part, 1) for part in w_parts]
    whole = call(
        join_weight_body,
        [sds((NZ, 4, 2 * HALF, 2 * KVH * HD), bf16)],
        [SMEM] + [ANY] * 8,
        0,
        21 << 20,
        scratch=[pltpu.SemaphoreType.DMA((8,))],
        vmem=24,
    )(info, *w_parts)[0]
    kv_near = swap(jnp.concatenate([kv_rows[ROWS : 2 * ROWS], kv_far[ROWS:]], axis=0), 1)

    quarter = sds((ROWS, QUARTER), bf16)
    res = call(
        final_body,
        [quarter] * 4 + [sds((1, D), f32)],
        [SMEM] + [VMEM] * 6,
        2 * ROWS * D * 1024,
        12 << 20,
        scratch=[
            pltpu.VMEM((4, ROWS, QUARTER), f32),
            pltpu.VMEM((ROWS, 2 * KVH * HD), bf16),
        ],
        vmem=24,
    )(info, kv_rows, kv_far, kv_near, trunk[0], gains, whole)
    dq_send, own = lax.optimization_barrier((dq[2], res[0]))
    total = own.astype(f32)
    for d in (1, 2, 3):
        total = total + lax.ppermute(
            res[d], "head", [(y, (y + d) % 4) for y in range(4)]
        ).astype(f32)
    trunk_grad = total.astype(bf16)

    gain = res[4].reshape(D // HD, HD)
    gain = gain + swap(gain, 1)
    beside = swap_x(gain, 1) + swap_x(gain, 3)
    gain = (gain + swap_x(gain, 2)) + beside
    spread = jnp.broadcast_to(gain[None], (NZ, D // HD, HD))
    gains_of_z = lax.all_to_all(spread, "z", 0, 0, tiled=True)
    dq_far = swap(dq_send, 2)
    dq_near = swap(jnp.concatenate([dq[1], dq_far[ROWS:]], axis=0), 1)
    query_grad = call(
        join_q_body, [sds((ROWS, QH * HD), bf16)], [SMEM] + [VMEM] * 3, 0, 1 << 20
    )(info, dq[0], dq_far, dq_near)[0]
    gains_of_z, query_grad = lax.optimization_barrier((gains_of_z, query_grad))
    gain = jnp.sum(gains_of_z, axis=0)
    return (query_grad[None, None], trunk_grad[None], gain.reshape(1, D))


def solution(mesh):
    cut = Mesh(
        mesh.devices.reshape(4, NZ, 2, 2, 2), ("head",) + SEQ + ("dp",)
    )
    placed = (
        P("dp", SEQ, None),
        P("head", None),
        P("head", "dp", SEQ, None),
        P("head", "dp", SEQ, None),
        P("head", "dp", SEQ, None),
        P("head", "dp", SEQ, None),
        P("head", "dp", SEQ, None),
        P("head", SEQ, None),
    )
    return jax.shard_map(
        per_device,
        mesh=cut,
        in_specs=placed,
        out_specs=(P("head", "dp", SEQ, None), P("dp", SEQ, "head"), P("head", None)),
        check_vma=False,
    )
```
